256 devices in a mesh: replica: 16 (over x, z_hi, core), fsdp: 16 (over z_lo, y).
Axes of the slice: x: 4, y: 4, z: 8 (z_hi: 2, z_lo: 4; z = z_hi * 4 + z_lo), core: 2. Of those that a mesh axis runs over, the one named last changes fastest.
Arguments:
- activations: bfloat16 [16, 2048, 4096], P('replica', 'fsdp'), may hold values from -6 to 6
- cotangent: bfloat16 [16, 2048, 6144], P('replica', 'fsdp'), may hold values from -120 to 120
- local_weight: bfloat16 [16, 4096, 6144], P('replica', None, 'fsdp'), may hold values from -6 to 6
- outer_param: float32 [4096, 6144], P('replica', 'fsdp'), may hold values from -6 to 6
- outer_moment: float32 [4096, 6144], P('replica', 'fsdp'), may hold values from -4 to 4
Outputs:
- merged_weight: bfloat16 [16, 4096, 6144], P('replica', None, 'fsdp')
- param_new: float32 [4096, 6144], P('replica', 'fsdp')
- moment_new: float32 [4096, 6144], P('replica', 'fsdp')
The draws below stay inside these ranges and needn't reach their ends.
All inputs are finite; a program needn't handle non-finite values.
Results may differ from the reference program's by a relative error of at most 0.01.
Values may be sent and summed in bfloat16 or wider, within the bound.
A program may use at most 128 MiB of HBM per device.

```python
import math
import jax
import jax.numpy as jnp
from jax import lax

D = 4096
FF = 6144
REPLICAS = 16
TOKENS = 2048


def draw_cotangent(key, part):
    key = jax.random.fold_in(key, 7)
    first, second, third = jax.random.split(key, 3)
    shape = (REPLICAS, TOKENS, FF)
    base = jax.random.normal(first, shape, jnp.float32)
    base = jnp.clip(base, -4.0, 4.0)
    row_scale = jnp.exp(jax.random.uniform(second, (REPLICAS, TOKENS, 1), jnp.float32, 0.0, math.log(10.0)))
    place = jnp.arange(FF, dtype=jnp.float32) / FF
    col_scale = jnp.exp(jax.random.uniform(third, (1, 1, FF), jnp.float32, 0.0, math.log(10.0)) + math.log(3.0) * place[None, None, :])
    return jnp.clip(base * row_scale * col_scale, -120.0, 120.0).astype(jnp.bfloat16)


def spiked(drawn, rng, source, target, shards_of, factor):
    def block_of(axis_at):
        return (jnp.arange(drawn.shape[axis_at]) // (drawn.shape[axis_at] // shards_of)).reshape((-1,) + (1,) * (drawn.ndim - 1 - axis_at))

    one_side = jax.random.permutation(rng, shards_of)[block_of(target)]
    other_side = (block_of(target) + shards_of // 2) % shards_of
    return jnp.where((block_of(source) == one_side) | (block_of(source) == other_side), factor * drawn, drawn)


def level_of(rng, dims, cuts, least, largest):
    gain = 1.0
    for position, blocks in cuts:
        draws = jax.random.uniform(jax.random.fold_in(jax.random.fold_in(rng, 6), position), (blocks,), jnp.float32, least / len(cuts), largest / len(cuts))
        gain = gain * jnp.repeat(jnp.exp(draws), dims[position] // blocks).reshape((-1,) + (1,) * (len(dims) - 1 - position))
    return gain


def normal_values(key, shape, width, reach, shards=(), kind=jnp.bfloat16):
    drawn = width * jax.random.normal(key, shape, jnp.float32)
    if shards:
        drawn = drawn * level_of(key, shape, shards, -0.22, 0.18)
    return jnp.clip(drawn, -reach, reach).astype(kind)


def bell_draw_with(key, extent, scale, bound, pieces, heavy, kind=jnp.bfloat16):
    entries = scale * jax.random.normal(key, extent, jnp.float32)
    if pieces:
        entries = entries * level_of(key, extent, pieces, -0.22, 0.18)
    return jnp.clip(spiked(entries, jax.random.fold_in(key, 3), *heavy), -bound, bound).astype(kind)


def setup_inputs(seed: int = 0) -> dict:
    splits = jax.random.split(jax.random.key(seed), 6)
    activations = normal_values(splits[0], (REPLICAS, TOKENS, D), 1.0, 6.0, ((0, 16), (1, 16)))
    cotangent = draw_cotangent(jax.random.fold_in(splits[5], 71), 0)
    local_weight = bell_draw_with(splits[2], (REPLICAS, D, FF), 1.0, 6.0, ((0, 16), (2, 16)), (0, 1, 16, 2.0))
    outer_param = normal_values(splits[3], (D, FF), 1.0, 6.0, ((0, 16), (1, 16)), jnp.float32)
    outer_moment = normal_values(splits[4], (D, FF), 0.5, 4.0, ((0, 16), (1, 16)), jnp.float32)
    return dict(activations=activations, cotangent=cotangent, local_weight=local_weight, outer_param=outer_param, outer_moment=outer_moment)


def reference(activations, cotangent, local_weight, outer_param, outer_moment):
    summed = lax.optimization_barrier(jnp.sum(local_weight.astype(jnp.float32), axis=0))
    delta = outer_param - summed / REPLICAS
    moment_new = 0.9 * outer_moment + delta
    param_new = outer_param - 0.7 * (delta + 0.9 * moment_new)
    param_low = param_new.astype(jnp.bfloat16)

    def one_replica(items):
        inputs, grads, weight = items
        gradient = jnp.dot(inputs.T, grads, preferred_element_type=jnp.float32)
        spread = jnp.sqrt(jnp.mean(gradient * gradient) + 1e-06)
        stepped = weight.astype(jnp.float32) - 0.25 * gradient / spread
        return (0.5 * stepped + 0.5 * param_low.astype(jnp.float32)).astype(jnp.bfloat16)
    merged_weight = lax.map(one_replica, (activations, cotangent, local_weight))
    return (merged_weight, param_new, moment_new)
```

```python
import functools

import jax
import jax.numpy as jnp
from jax import lax
from jax.experimental import pallas as pl
from jax.experimental.pallas import tpu as pltpu
from jax.sharding import PartitionSpec as P

MESH = pl.DeviceIdType.MESH
F32, BF16 = jnp.float32, jnp.bfloat16

NX, NH, NC, NZ, NY = 4, 2, 2, 4, 4
TOK, D, FF = 128, 4096, 6144
ROWS, COLS = D // NY, FF // NZ
OWN = COLS // NY
BLOCK = 256
CHUNKS = (256, 256, 256, 128, 128)
STARTS = tuple(sum(CHUNKS[:q]) for q in range(len(CHUNKS)))
Q = len(CHUNKS)


def kernel(act, cot, lw, op, om, merged, pn_out, mn_out, *scratch):
    at = scratch[:Q]
    (
        act_v, act_t, cb, gs, gr, lw_v, rsc, rss, rsx, zs, zr, part, plow, op_v, om_v, pn_v, mn_v, out_v,
        sq, sq_y, sq_z,
        loc, out_sem, a1s, a1r, a2us, a2ur, a2ds, a2dr, c1s, c1r, c2s, c2r, gss, grs,
        rcs, rcr, rxs, rxr, zhs, zhr, gzs, gzr, gxs, gxr, gcs, gcr, qys, qyr, qzs, qzr,
    ) = scratch[Q:]
    rep, fs = lax.axis_index("replica"), lax.axis_index("fsdp")
    x, zh, c = rep // 4, (rep // 2) % 2, rep % 2
    z, y = fs // 4, fs % 4

    def at_y(k):
        return (rep, z * 4 + (y + k) % 4)

    def at_z(k):
        return (rep, ((z + k) % 4) * 4 + y)

    def at_x(k):
        return (((x + k) % 4) * 4 + zh * 2 + c, fs)

    at_c = (x * 4 + zh * 2 + (1 - c), fs)
    at_h = (x * 4 + (1 - zh) * 2 + c, fs)
    up, down = (rep, lax.min(z + 1, 3) * 4 + y), (rep, lax.max(z - 1, 0) * 4 + y)

    def remote(src, dst, ss, rs, dev):
        return pltpu.make_async_remote_copy(src_ref=src, dst_ref=dst, send_sem=ss, recv_sem=rs, device_id=dev, device_id_type=MESH)

    def landed(dst, ss, rs):
        remote(dst, dst, ss, rs, at_c).wait_recv()

    barrier = pltpu.get_barrier_semaphore()
    peers = [at_y(k) for k in (1, 2, 3)] + [at_z(k) for k in (1, 2, 3)] + [at_x(k) for k in (1, 2, 3)] + [at_c, at_h]
    for dev in peers:
        pl.semaphore_signal(barrier, inc=1, device_id=dev, device_id_type=MESH)
    act_in = pltpu.make_async_copy(act, act_v, loc.at[0])
    act_in.start()
    lw_in = pltpu.make_async_copy(lw, lw_v, loc.at[1])
    lw_in.start()
    op_in = pltpu.make_async_copy(op, op_v, loc.at[2])
    op_in.start()
    om_in = pltpu.make_async_copy(om, om_v, loc.at[3])
    om_in.start()

    def cot_cols(zt):
        return cot.at[:, pl.ds(pl.multiple_of(zt * COLS, COLS), COLS)]

    def cb_slot(zt, yt):
        return cb.at[zt, pl.ds(pl.multiple_of(yt * TOK, TOK), TOK)]

    cot_in = pltpu.make_async_copy(cot_cols(z), cb_slot(z, y), loc.at[4])
    cot_in.start()
    pl.semaphore_wait(barrier, len(peers))

    sends = []

    def send(*args):
        cp = remote(*args)
        cp.start()
        sends.append(cp)

    for k in (2, 1, 3):
        send(cot_cols((z + k) % 4), cb_slot(z, y), c1s.at[k - 1], c1r.at[k - 1], at_z(k))
    send(lw.at[:, 1 - c], rsc, rcs, rcr, at_c)

    act_in.wait()

    def at_cols(q, zt, yt):
        return at[q].at[zt, :, pl.ds(pl.multiple_of(yt * TOK, TOK), TOK)]

    for q in range(Q):
        size, start = CHUNKS[q], STARTS[q]
        for k in (2, 1, 3, 0):
            col = pl.multiple_of(((y + k) % 4) * ROWS + start, 128)
            block = act_v[:, pl.ds(col, size)].T
            if k == 0:
                at[q][z, :, pl.ds(pl.multiple_of(y * TOK, TOK), TOK)] = block
            else:
                act_t[k - 1, pl.ds(start, size)] = block
                send(act_t.at[k - 1, pl.ds(start, size)], at_cols(q, z, y), a1s.at[q, k - 1], a1r.at[q, k - 1], at_y(k))

    for k in (2, 1, 3):
        send(cot_cols(z), cb_slot(z, y), c2s.at[0, k - 1], c2r.at[0, k - 1], at_y(k))

    lw_in.wait()
    landed(rsc, rcs, rcr)

    @pl.loop(0, NX * NH)
    def _(i):
        rss[i] = (lw_v[i, c].astype(F32) + rsc[i].astype(F32)).astype(BF16)

    for k in (2, 1, 3):
        send(rss.at[pl.ds(2 * ((x + k) % 4), 2)], rsx.at[pl.ds(2 * x, 2)], rxs.at[k - 1], rxr.at[k - 1], at_x(k))

    for q in range(Q):
        for k in (1, 2, 3):
            landed(at_cols(q, z, (y + 4 - k) % 4), a1s.at[q, k - 1], a1r.at[q, k - 1])

        @pl.when(z < 3)
        def _():
            remote(at[q].at[z], at[q].at[z], a2us.at[q, 0], a2ur.at[q, 0], up).start()

        @pl.when(z > 0)
        def _():
            remote(at[q].at[z], at[q].at[z], a2ds.at[q, 0], a2dr.at[q, 0], down).start()

    for k in (1, 2, 3):
        landed(rsx.at[pl.ds(2 * ((x + 4 - k) % 4), 2)], rxs.at[k - 1], rxr.at[k - 1])

    def over_x(h):
        total = rss[2 * x + h].astype(F32)
        for k in (1, 2, 3):
            total += rsx[2 * ((x + k) % 4) + h].astype(F32)
        return total

    zs[...] = over_x(1 - zh).astype(BF16)
    send(zs, zr, zhs, zhr, at_h)
    part[...] = over_x(zh)

    cot_in.wait()
    for k in (1, 3, 2):
        zt = (z + 4 - k) % 4
        landed(cb_slot(zt, y), c1s.at[k - 1], c1r.at[k - 1])
        for j in (2, 1, 3):
            send(cb_slot(zt, y), cb_slot(zt, y), c2s.at[k, j - 1], c2r.at[k, j - 1], at_y(j))

    def forward(q):
        for d in (1, 2, 3):

            @pl.when(z >= d)
            def _():
                slot = at[q].at[lax.max(z - d, 0)]
                landed(slot, a2us.at[q, d - 1], a2ur.at[q, d - 1])
                if d < 3:

                    @pl.when(z < 3)
                    def _():
                        remote(slot, slot, a2us.at[q, d], a2ur.at[q, d], up).start()

            @pl.when(z <= 3 - d)
            def _():
                slot = at[q].at[lax.min(z + d, 3)]
                landed(slot, a2ds.at[q, d - 1], a2dr.at[q, d - 1])
                if d < 3:

                    @pl.when(z > 0)
                    def _():
                        remote(slot, slot, a2ds.at[q, d], a2dr.at[q, d], down).start()

    def forwarded(q):
        for d in (0, 1, 2):

            @pl.when((z < 3) & (z >= d))
            def _():
                slot = at[q].at[lax.max(z - d, 0)]
                remote(slot, slot, a2us.at[q, d], a2ur.at[q, d], up).wait_send()

            @pl.when((z > 0) & (z <= 3 - d))
            def _():
                slot = at[q].at[lax.min(z + d, 3)]
                remote(slot, slot, a2ds.at[q, d], a2dr.at[q, d], down).wait_send()

    def plow_at(xt, ht, ct):
        return plow.at[xt * 2 + ht, ct]

    def update():
        op_in.wait()
        om_in.wait()
        landed(zr, zhs, zhr)
        outer = op_v[...]
        delta = outer - (part[...] + zr[...].astype(F32)) * (1.0 / 16.0)
        moment = 0.9 * om_v[...] + delta
        param = outer - 0.7 * (delta + 0.9 * moment)
        mn_v[...] = moment
        pn_v[...] = param
        plow[x * 2 + zh, c] = param.astype(BF16)
        mine = plow_at(x, zh, c)
        send(mine, mine, gzs, gzr, at_h)
        for k in (2, 1, 3):
            send(mine, mine, gxs.at[0, k - 1], gxr.at[0, k - 1], at_x(k))
        for v, o, s in ((pn_v, pn_out, 5), (mn_v, mn_out, 6)):
            pltpu.make_async_copy(v, o, loc.at[s]).start()

    def spread_h():
        other = plow_at(x, 1 - zh, c)
        landed(other, gzs, gzr)
        for k in (2, 1, 3):
            send(other, other, gxs.at[1, k - 1], gxr.at[1, k - 1], at_x(k))

    def spread_c():
        for h in (0, 1):
            for k in (1, 2, 3):
                landed(plow_at((x + 4 - k) % 4, zh if h == 0 else 1 - zh, c), gxs.at[h, k - 1], gxr.at[h, k - 1])
        send(plow.at[:, c], plow.at[:, c], gcs, gcr, at_c)

    def gr_rows(yt, q):
        return gr.at[pl.ds(pl.multiple_of(yt * ROWS + STARTS[q], 128), CHUNKS[q])]

    sq[...] = jnp.zeros_like(sq)

    def gradient(q):
        size = CHUNKS[q]

        @pl.loop(0, NY)
        def _(i):
            j = (y + 1 + i) % 4
            cols = pl.ds(pl.multiple_of(j * OWN, OWN), OWN)
            total = jnp.zeros((size, OWN), F32)
            for g in range(NZ):
                total += jnp.dot(at[q][g], cb[g, :, cols], preferred_element_type=F32)
            sq[...] += jnp.sum((total * total).reshape(size // 8, 8, OWN), axis=0)
            gs[i, pl.ds(STARTS[q], size)] = total.astype(BF16)

            @pl.when(i < 3)
            def _():
                remote(gs.at[i, pl.ds(STARTS[q], size)], gr_rows(y, q), gss.at[q, i], grs.at[q, i], (rep, z * 4 + j)).start()

        gr[pl.ds(pl.multiple_of(y * ROWS + STARTS[q], 128), size)] = gs[3, pl.ds(STARTS[q], size)]

    def gathered_c():
        for s in range(4):
            zt = (z + 4 - s) % 4
            for j in (1, 2, 3):
                landed(cb_slot(zt, (y + 4 - j) % 4), c2s.at[s, j - 1], c2r.at[s, j - 1])

    forward(0)
    update()
    forward(1)
    spread_h()
    forward(2)
    gathered_c()
    gradient(0)
    forward(3)
    gradient(1)
    spread_c()
    forward(4)
    gradient(2)
    gradient(3)
    gradient(4)

    for k in (1, 2, 3):
        send(sq, sq_y.at[k - 1], qys.at[k - 1], qyr.at[k - 1], at_y(k))
    for k in (1, 2, 3):
        landed(sq_y.at[k - 1], qys.at[k - 1], qyr.at[k - 1])
    sq_z[3] = sq[...] + sq_y[0] + sq_y[1] + sq_y[2]
    for k in (1, 2, 3):
        send(sq_z.at[3], sq_z.at[k - 1], qzs.at[k - 1], qzr.at[k - 1], at_z(k))
    for k in (1, 2, 3):
        landed(sq_z.at[k - 1], qzs.at[k - 1], qzr.at[k - 1])
    square = jnp.sum(sq_z[0] + sq_z[1] + sq_z[2] + sq_z[3], axis=(0, 1), keepdims=True)
    scale = 0.125 / jnp.sqrt(square * (1.0 / (D * FF)) + 1e-6)

    landed(plow.at[:, 1 - c], gcs, gcr)
    for q in range(Q):
        for i in range(3):
            landed(gr_rows((y + 3 - i) % 4, q), gss.at[q, i], grs.at[q, i])

    @pl.loop(0, D // BLOCK)
    def _(b):
        rows = pl.ds(pl.multiple_of(b * BLOCK, BLOCK), BLOCK)
        base = lw_v[b // 2, b % 2].astype(F32) + plow[b // 2, b % 2].astype(F32)
        out_v[rows] = (0.5 * base - scale * gr[rows].astype(F32)).astype(BF16)
        pltpu.make_async_copy(out_v.at[rows], merged.at[rows], out_sem).start()

    for cp in sends:
        cp.wait_send()
    for q in range(Q):
        forwarded(q)
        for i in range(3):
            j = (y + 1 + i) % 4
            remote(gs.at[i, pl.ds(STARTS[q], CHUNKS[q])], gr_rows(y, q), gss.at[q, i], grs.at[q, i], (rep, z * 4 + j)).wait_send()
    for v, o, s in ((pn_v, pn_out, 5), (mn_v, mn_out, 6)):
        pltpu.make_async_copy(v, o, loc.at[s]).wait()
    pltpu.make_async_copy(out_v, merged, out_sem).wait()


def local(activations, cotangent, local_weight, outer_param, outer_moment):
    dma = pltpu.SemaphoreType.DMA
    state = (BLOCK, OWN)
    half = (NX * NH, BLOCK, OWN)
    whole = (NX * NH, NC, BLOCK, OWN)
    scratch = [pltpu.VMEM((NZ, size, NY * TOK), BF16) for size in CHUNKS]
    scratch += [
        pltpu.VMEM((TOK, D), BF16),
        pltpu.VMEM((3, ROWS, TOK), BF16),
        pltpu.VMEM((NZ, NY * TOK, COLS), BF16),
        pltpu.VMEM((NY, ROWS, OWN), BF16),
        pltpu.VMEM((D, OWN), BF16),
        pltpu.VMEM(whole, BF16),
        pltpu.VMEM(half, BF16),
        pltpu.VMEM(half, BF16),
        pltpu.VMEM(half, BF16),
        pltpu.VMEM(state, BF16),
        pltpu.VMEM(state, BF16),
        pltpu.VMEM(state, F32),
        pltpu.VMEM(whole, BF16),
        pltpu.VMEM(state, F32),
        pltpu.VMEM(state, F32),
        pltpu.VMEM(state, F32),
        pltpu.VMEM(state, F32),
        pltpu.VMEM((D, OWN), BF16),
        pltpu.VMEM((8, OWN), F32),
        pltpu.VMEM((3, 8, OWN), F32),
        pltpu.VMEM((4, 8, OWN), F32),
    ]
    scratch += [dma((7,)), dma(())]
    scratch += [dma((Q, 3))] * 6
    scratch += [dma((3,))] * 2 + [dma((4, 3))] * 2 + [dma((Q, 3))] * 2
    scratch += [dma(())] * 2 + [dma((3,))] * 2 + [dma(())] * 4
    scratch += [dma((2, 3))] * 2 + [dma(())] * 2 + [dma((3,))] * 4
    merged, param_new, moment_new = pl.pallas_call(
        kernel,
        out_shape=(
            jax.ShapeDtypeStruct((D, OWN), BF16),
            jax.ShapeDtypeStruct(state, F32),
            jax.ShapeDtypeStruct(state, F32),
        ),
        in_specs=[pl.BlockSpec(memory_space=pl.ANY)] * 5,
        out_specs=[pl.BlockSpec(memory_space=pl.ANY)] * 3,
        scratch_shapes=scratch,
        compiler_params=pltpu.CompilerParams(collective_id=0, has_side_effects=True, vmem_limit_bytes=60 * 2**20),
        name="merge",
    )(activations[0], cotangent[0], local_weight.reshape(whole), outer_param, outer_moment)
    return (merged[None], param_new, moment_new)


def solution(mesh):
    placed = (
        P("replica", "fsdp", None),
        P("replica", "fsdp", None),
        P("replica", None, "fsdp"),
        P("replica", "fsdp"),
        P("replica", "fsdp"),
    )
    return jax.shard_map(
        local,
        mesh=mesh,
        in_specs=placed,
        out_specs=(P("replica", None, "fsdp"), P("replica", "fsdp"), P("replica", "fsdp")),
        check_vma=False,
    )
```

```python
import functools

import jax
import jax.numpy as jnp
from jax import lax
from jax.experimental import pallas as pl
from jax.experimental.pallas import tpu as pltpu
from jax.sharding import PartitionSpec as P

MESH = pl.DeviceIdType.MESH
F32, BF16 = jnp.float32, jnp.bfloat16

NX, NH, NC, NZ, NY = 4, 2, 2, 4, 4
TOK, D, FF = 128, 4096, 6144
ROWS, COLS = D // NY, FF // NZ
OWN = COLS // NY
BLOCK = 256
CHUNKS = (256, 256, 256, 128, 128)
STARTS = tuple(sum(CHUNKS[:q]) for q in range(len(CHUNKS)))
Q = len(CHUNKS)


def kernel(act, cot, lw, op, om, merged, pn_out, mn_out, *scratch):
    at = scratch[:Q]
    (
        act_v, act_t, cb, gs, gr, lw_v, rsc, rss, rsx, zs, zr, part, plow, op_v, om_v, pn_v, mn_v, out_v,
        sq, sqs, acc,
        loc, out_sem, a1s, a1r, a2us, a2ur, a2ds, a2dr, c1s, c1r, c2s, c2r, gss, grs,
        rcs, rcr, rxs, rxr, zhs, zhr, gzs, gzr, gxs, gxr, gcs, gcr, qss, qsr,
    ) = scratch[Q:]
    rep, fs = lax.axis_index("replica"), lax.axis_index("fsdp")
    x, zh, c = rep // 4, (rep // 2) % 2, rep % 2
    z, y = fs // 4, fs % 4

    def at_y(k):
        return (rep, z * 4 + (y + k) % 4)

    def in_plane(k):
        return (rep, ((z + k // 4) % 4) * 4 + (y + k % 4) % 4)

    def at_x(k):
        return (((x + k) % 4) * 4 + zh * 2 + c, fs)

    at_c = (x * 4 + zh * 2 + (1 - c), fs)
    at_h = (x * 4 + (1 - zh) * 2 + c, fs)
    up, down = (rep, lax.min(z + 1, 3) * 4 + y), (rep, lax.max(z - 1, 0) * 4 + y)

    def remote(src, dst, ss, rs, dev):
        return pltpu.make_async_remote_copy(src_ref=src, dst_ref=dst, send_sem=ss, recv_sem=rs, device_id=dev, device_id_type=MESH)

    def landed(dst, ss, rs):
        remote(dst, dst, ss, rs, at_c).wait_recv()

    barrier = pltpu.get_barrier_semaphore()
    others = range(1, NZ * NY)
    peers = [in_plane(k) for k in others] + [at_x(k) for k in (1, 2, 3)] + [at_c, at_h]
    for dev in peers:
        pl.semaphore_signal(barrier, inc=1, device_id=dev, device_id_type=MESH)
    act_in = pltpu.make_async_copy(act, act_v, loc.at[0])
    act_in.start()
    lw_in = pltpu.make_async_copy(lw, lw_v, loc.at[1])
    lw_in.start()
    op_in = pltpu.make_async_copy(op, op_v, loc.at[2])
    op_in.start()
    om_in = pltpu.make_async_copy(om, om_v, loc.at[3])
    om_in.start()

    def cot_cols(zt):
        return cot.at[:, pl.ds(pl.multiple_of(zt * COLS, COLS), COLS)]

    def cb_slot(zt, yt):
        return cb.at[zt, pl.ds(pl.multiple_of(yt * TOK, TOK), TOK)]

    cot_in = pltpu.make_async_copy(cot_cols(z), cb_slot(z, y), loc.at[4])
    cot_in.start()
    pl.semaphore_wait(barrier, len(peers))

    sends = []

    def send(*args):
        cp = remote(*args)
        cp.start()
        sends.append(cp)

    planes = (z, 1 + z % 2, (2 + 3 * z) % 5, 3 - 3 * (z // 2))

    def plane_dev(i):
        return (rep, planes[i] * 4 + y)

    def c1_send(i):
        send(cot_cols(planes[i]), cb_slot(z, y), c1s.at[i - 1], c1r.at[z], plane_dev(i))

    def c1_land(i):
        landed(cb_slot(planes[i], y), c1s.at[i - 1], c1r.at[planes[i]])

    def cb_half(zt, yt, h):
        return cb.at[zt, pl.ds(pl.multiple_of(yt * TOK + h * (TOK // 2), TOK // 2), TOK // 2)]

    def c2_send(s):
        src = cot_cols(z) if s == 0 else cb_slot(planes[s], y)
        send(src, cb_slot(planes[s], y), c2s.at[s, 0], c2r.at[s, 0], at_y(1))
        send(src, cb_slot(planes[s], y), c2s.at[s, 1], c2r.at[s, 1], at_y(3))

    def c2_pass(s):
        for i, k in ((0, 3), (1, 1)):
            landed(cb_slot(planes[s], (y + k) % 4), c2s.at[s, i], c2r.at[s, i])
            piece = cb_half(planes[s], (y + k) % 4, i)
            send(piece, piece, c2s.at[s, 2 + i], c2r.at[s, 2 + i], at_y(4 - k))

    def c2_land(s):
        for i in (0, 1):
            landed(cb_half(planes[s], (y + 2) % 4, i), c2s.at[s, 2 + i], c2r.at[s, 2 + i])

    def at_cols(q, zt, yt):
        return at[q].at[zt, :, pl.ds(pl.multiple_of(yt * TOK, TOK), TOK)]

    def a1_in():
        act_in.wait()

    def a1_send(q):
        size, start = CHUNKS[q], STARTS[q]
        for k in (2, 1, 3, 0):
            col = pl.multiple_of(((y + k) % 4) * ROWS + start, 128)
            block = act_v[:, pl.ds(col, size)].T
            if k == 0:
                at[q][z, :, pl.ds(pl.multiple_of(y * TOK, TOK), TOK)] = block
            else:
                act_t[k - 1, pl.ds(start, size)] = block
                send(act_t.at[k - 1, pl.ds(start, size)], at_cols(q, z, y), a1s.at[q, k - 1], a1r.at[q, k - 1], at_y(k))

    def a1_land(q):
        for k in (1, 2, 3):
            landed(at_cols(q, z, (y + 4 - k) % 4), a1s.at[q, k - 1], a1r.at[q, k - 1])

    def own_up(q):
        remote(at[q].at[z], at[q].at[z], a2us.at[q, 0], a2ur.at[q, 0], up).start()

    def own_down(q):
        remote(at[q].at[z], at[q].at[z], a2ds.at[q, 0], a2dr.at[q, 0], down).start()

    def own_out(q):
        pl.when((z == 0) | (z == 2))(lambda: own_up(q))
        pl.when((z == 1) | (z == 3))(lambda: own_down(q))

    def own_in(q):
        pl.when(z == 1)(lambda: own_up(q))
        pl.when(z == 2)(lambda: own_down(q))

    def rs_core():
        send(lw.at[:, 1 - c], rsc, rcs, rcr, at_c)

    def rs_x():
        lw_in.wait()
        landed(rsc, rcs, rcr)

        @pl.loop(0, NX * NH)
        def _(i):
            rss[i] = (lw_v[i, c].astype(F32) + rsc[i].astype(F32)).astype(BF16)

        for k in (2, 1, 3):
            send(rss.at[pl.ds(2 * ((x + k) % 4), 2)], rsx.at[pl.ds(2 * x, 2)], rxs.at[k - 1], rxr.at[k - 1], at_x(k))

    def over_x(h):
        total = rss[2 * x + h].astype(F32)
        for k in (1, 2, 3):
            total += rsx[2 * ((x + k) % 4) + h].astype(F32)
        return total

    def rs_h():
        for k in (1, 2, 3):
            landed(rsx.at[pl.ds(2 * ((x + 4 - k) % 4), 2)], rxs.at[k - 1], rxr.at[k - 1])
        zs[...] = over_x(1 - zh).astype(BF16)
        send(zs, zr, zhs, zhr, at_h)
        part[...] = over_x(zh)

    def from_below(q, d):
        slot = at[q].at[lax.max(z - d, 0)]
        landed(slot, a2us.at[q, d - 1], a2ur.at[q, d - 1])
        return slot

    def from_above(q, d):
        slot = at[q].at[lax.min(z + d, 3)]
        landed(slot, a2ds.at[q, d - 1], a2dr.at[q, d - 1])
        return slot

    def pass_up(q, d):
        slot = from_below(q, d)
        remote(slot, slot, a2us.at[q, d], a2ur.at[q, d], up).start()

    def pass_down(q, d):
        slot = from_above(q, d)
        remote(slot, slot, a2ds.at[q, d], a2dr.at[q, d], down).start()

    def pass_in(q):
        pl.when(z == 1)(lambda: pass_up(q, 1))
        pl.when(z == 2)(lambda: pass_down(q, 1))

    def pass_out(q, d):
        pl.when(z == 2)(lambda: pass_up(q, d))
        pl.when(z == 1)(lambda: pass_down(q, d))

    def a2_land(q):
        @pl.when(z == 3)
        def _():
            for d in (1, 2, 3):
                from_below(q, d)

        @pl.when(z == 0)
        def _():
            for d in (1, 2, 3):
                from_above(q, d)

    def forwarded(q):
        for d in (0, 1, 2):

            @pl.when((z < 3) & (z >= d))
            def _():
                slot = at[q].at[lax.max(z - d, 0)]
                remote(slot, slot, a2us.at[q, d], a2ur.at[q, d], up).wait_send()

            @pl.when((z > 0) & (z <= 3 - d))
            def _():
                slot = at[q].at[lax.min(z + d, 3)]
                remote(slot, slot, a2ds.at[q, d], a2dr.at[q, d], down).wait_send()

    def plow_at(xt, ht, ct):
        return plow.at[xt * 2 + ht, ct]

    def update():
        op_in.wait()
        om_in.wait()
        landed(zr, zhs, zhr)
        outer = op_v[...]
        delta = outer - (part[...] + zr[...].astype(F32)) * (1.0 / 16.0)
        moment = 0.9 * om_v[...] + delta
        param = outer - 0.7 * (delta + 0.9 * moment)
        mn_v[...] = moment
        pn_v[...] = param
        plow[x * 2 + zh, c] = param.astype(BF16)
        mine = plow_at(x, zh, c)
        send(mine, mine, gzs, gzr, at_h)
        for k in (2, 1, 3):
            send(mine, mine, gxs.at[0, k - 1], gxr.at[0, k - 1], at_x(k))
        for v, o, s in ((pn_v, pn_out, 5), (mn_v, mn_out, 6)):
            pltpu.make_async_copy(v, o, loc.at[s]).start()

    def spread_h():
        other = plow_at(x, 1 - zh, c)
        landed(other, gzs, gzr)
        for k in (2, 1, 3):
            send(other, other, gxs.at[1, k - 1], gxr.at[1, k - 1], at_x(k))

    def spread_c():
        for h in (0, 1):
            for k in (1, 2, 3):
                landed(plow_at((x + 4 - k) % 4, zh if h == 0 else 1 - zh, c), gxs.at[h, k - 1], gxr.at[h, k - 1])
        send(plow.at[:, c], plow.at[:, c], gcs, gcr, at_c)

    def gr_rows(yt, q):
        return gr.at[pl.ds(pl.multiple_of(yt * ROWS + STARTS[q], 128), CHUNKS[q])]

    def gradient(q):
        if q == 0:
            cot_in.wait()
        size = CHUNKS[q]
        rows = pl.ds(0, size)
        for g in range(NZ):
            term = jnp.dot(at[q][g], cb[g], preferred_element_type=F32)
            if g == 0:
                acc[rows] = term
            else:
                acc[rows] += term

        @pl.loop(0, NY)
        def _(i):
            j = (y + 1 + i) % 4
            total = acc[rows, pl.ds(pl.multiple_of(j * OWN, OWN), OWN)]
            sq[...] += jnp.sum((total * total).reshape(size // 8, 8, OWN), axis=0)
            gs[i, pl.ds(STARTS[q], size)] = total.astype(BF16)

        gr[pl.ds(pl.multiple_of(y * ROWS + STARTS[q], 128), size)] = gs[3, pl.ds(STARTS[q], size)]

    def g_send(q):
        for i in (1, 0, 2):
            send(gs.at[i, pl.ds(STARTS[q], CHUNKS[q])], gr_rows(y, q), gss.at[q, i], grs.at[q, i], at_y(i + 1))

    def g_land(q):
        for i in range(3):
            landed(gr_rows((y + 3 - i) % 4, q), gss.at[q, i], grs.at[q, i])

    def squares_send():
        for i, k in enumerate(others):
            send(sq, sqs.at[i], qss.at[i], qsr.at[i], in_plane(k))

    def squares_land():
        for i in range(len(others)):
            landed(sqs.at[i], qss.at[i], qsr.at[i])

    def finish():
        square = sq[...]
        for i in range(len(others)):
            square += sqs[i]
        square = jnp.sum(square, axis=(0, 1), keepdims=True)
        scale = 0.125 / jnp.sqrt(square * (1.0 / (D * FF)) + 1e-6)

        landed(plow.at[:, 1 - c], gcs, gcr)

        @pl.loop(0, D // BLOCK)
        def _(b):
            rows = pl.ds(pl.multiple_of(b * BLOCK, BLOCK), BLOCK)
            base = lw_v[b // 2, b % 2].astype(F32) + plow[b // 2, b % 2].astype(F32)
            out_v[rows] = (0.5 * base - scale * gr[rows].astype(F32)).astype(BF16)
            pltpu.make_async_copy(out_v.at[rows], merged.at[rows], out_sem).start()

    sq[...] = jnp.zeros_like(sq)
    steps = [
        (c1_send, 1), (c1_send, 2), (c1_send, 3), (rs_core,), (a1_in,), (a1_send, 0), (a1_send, 1), (a1_send, 2), (a1_send, 3), (a1_send, 4),
        (c2_send, 0), (rs_x,), (a1_land, 0), (own_out, 0), (own_in, 0), (a1_land, 1), (own_out, 1), (a1_land, 2), (own_out, 2), (a1_land, 3), (own_out, 3), (a1_land, 4), (own_out, 4),
        (c1_land, 1), (c2_send, 1), (c2_pass, 0), (rs_h,), (c1_land, 2), (c2_send, 2), (pass_in, 0), (own_in, 1), (c1_land, 3), (c2_send, 3), (pass_in, 1), (own_in, 2),
        (c2_pass, 1), (pass_out, 0, 1), (pass_in, 2), (own_in, 3), (pass_out, 0, 2), (update,), (c2_pass, 2), (pass_out, 1, 1), (pass_in, 3), (own_in, 4), (pass_out, 1, 2), (pass_in, 4),
        (c2_pass, 3), (pass_out, 2, 1), (spread_h,), (pass_out, 2, 2), (pass_out, 3, 1),
        (c2_land, 0), (c2_land, 1), (c2_land, 2), (c2_land, 3), (a2_land, 0), (gradient, 0), (g_send, 0), (pass_out, 3, 2), (pass_out, 4, 1), (a2_land, 1), (gradient, 1), (g_send, 1), (pass_out, 4, 2),
        (spread_c,), (a2_land, 2), (gradient, 2), (g_send, 2), (a2_land, 3), (gradient, 3), (g_send, 3),
        (a2_land, 4), (gradient, 4), (squares_send,), (g_send, 4), (squares_land,), (g_land, 0), (g_land, 1), (g_land, 2), (g_land, 3), (g_land, 4), (finish,),
    ]
    for step, *args in steps:
        step(*args)

    for cp in sends:
        cp.wait_send()
    for q in range(Q):
        forwarded(q)
    for v, o, s in ((pn_v, pn_out, 5), (mn_v, mn_out, 6)):
        pltpu.make_async_copy(v, o, loc.at[s]).wait()
    pltpu.make_async_copy(out_v, merged, out_sem).wait()


def local(activations, cotangent, local_weight, outer_param, outer_moment):
    dma = pltpu.SemaphoreType.DMA
    state = (BLOCK, OWN)
    half = (NX * NH, BLOCK, OWN)
    whole = (NX * NH, NC, BLOCK, OWN)
    scratch = [pltpu.VMEM((NZ, size, NY * TOK), BF16) for size in CHUNKS]
    scratch += [
        pltpu.VMEM((TOK, D), BF16),
        pltpu.VMEM((3, ROWS, TOK), BF16),
        pltpu.VMEM((NZ, NY * TOK, COLS), BF16),
        pltpu.VMEM((NY, ROWS, OWN), BF16),
        pltpu.VMEM((D, OWN), BF16),
        pltpu.VMEM(whole, BF16),
        pltpu.VMEM(half, BF16),
        pltpu.VMEM(half, BF16),
        pltpu.VMEM(half, BF16),
        pltpu.VMEM(state, BF16),
        pltpu.VMEM(state, BF16),
        pltpu.VMEM(state, F32),
        pltpu.VMEM(whole, BF16),
        pltpu.VMEM(state, F32),
        pltpu.VMEM(state, F32),
        pltpu.VMEM(state, F32),
        pltpu.VMEM(state, F32),
        pltpu.VMEM((D, OWN), BF16),
        pltpu.VMEM((8, OWN), F32),
        pltpu.VMEM((NZ * NY - 1, 8, OWN), F32),
        pltpu.VMEM((max(CHUNKS), COLS), F32),
    ]
    scratch += [dma((7,)), dma(())]
    scratch += [dma((Q, 3))] * 6
    scratch += [dma((3,)), dma((4,))] + [dma((4, 4))] * 2 + [dma((Q, 3))] * 2
    scratch += [dma(())] * 2 + [dma((3,))] * 2 + [dma(())] * 4
    scratch += [dma((2, 3))] * 2 + [dma(())] * 2 + [dma((NZ * NY - 1,))] * 2
    merged, param_new, moment_new = pl.pallas_call(
        kernel,
        out_shape=(
            jax.ShapeDtypeStruct((D, OWN), BF16),
            jax.ShapeDtypeStruct(state, F32),
            jax.ShapeDtypeStruct(state, F32),
        ),
        in_specs=[pl.BlockSpec(memory_space=pl.ANY)] * 5,
        out_specs=[pl.BlockSpec(memory_space=pl.ANY)] * 3,
        scratch_shapes=scratch,
        compiler_params=pltpu.CompilerParams(collective_id=0, has_side_effects=True, vmem_limit_bytes=60 * 2**20),
        name="merge",
    )(activations[0], cotangent[0], local_weight.reshape(whole), outer_param, outer_moment)
    return (merged[None], param_new, moment_new)


def solution(mesh):
    placed = (
        P("replica", "fsdp", None),
        P("replica", "fsdp", None),
        P("replica", None, "fsdp"),
        P("replica", "fsdp"),
        P("replica", "fsdp"),
    )
    return jax.shard_map(
        local,
        mesh=mesh,
        in_specs=placed,
        out_specs=(P("replica", None, "fsdp"), P("replica", "fsdp"), P("replica", "fsdp")),
        check_vma=False,
    )
```

```python
import functools

import jax
import jax.numpy as jnp
from jax import lax
from jax.experimental import pallas as pl
from jax.experimental.pallas import tpu as pltpu
from jax.sharding import PartitionSpec as P

MESH = pl.DeviceIdType.MESH
F32, BF16 = jnp.float32, jnp.bfloat16

NX, NH, NC, NZ, NY = 4, 2, 2, 4, 4
TOK, D, FF = 128, 4096, 6144
ROWS, COLS = D // NY, FF // NZ
OWN = COLS // NY
BLOCK = 256
PIECE = 256
CHUNKS = (128, 128, 128, 128, 128, 128, 128, 128)
STARTS = tuple(sum(CHUNKS[:q]) for q in range(len(CHUNKS)))
Q = len(CHUNKS)


def exchange(act, cot, lw, op, om, g_out, plow_out, scale_out, pn_out, mn_out, *scratch):
    at = scratch[:Q]
    (
        act_v, act_t, cb, gs, lw_v, rsc, rss, rsx, zs, zr, part, plow, op_v, om_v, pn_v, mn_v,
        sq, sqs, acc,
        loc, gos, a1s, a1r, a2us, a2ur, a2ds, a2dr, c1s, c1r, c2s, c2r, gss, grs,
        rcs, rcr, rxs, rxr, zhs, zhr, gzs, gzr, gxs, gxr, gcs, gcr, qss, qsr,
    ) = scratch[Q:]
    rep, fs = lax.axis_index("replica"), lax.axis_index("fsdp")
    x, zh, c = rep // 4, (rep // 2) % 2, rep % 2
    z, y = fs // 4, fs % 4

    def at_y(k):
        return (rep, z * 4 + (y + k) % 4)

    def in_plane(k):
        return (rep, ((z + k // 4) % 4) * 4 + (y + k % 4) % 4)

    def at_x(k):
        return (((x + k) % 4) * 4 + zh * 2 + c, fs)

    at_c = (x * 4 + zh * 2 + (1 - c), fs)
    at_h = (x * 4 + (1 - zh) * 2 + c, fs)
    up, down = (rep, lax.min(z + 1, 3) * 4 + y), (rep, lax.max(z - 1, 0) * 4 + y)

    def remote(src, dst, ss, rs, dev):
        return pltpu.make_async_remote_copy(src_ref=src, dst_ref=dst, send_sem=ss, recv_sem=rs, device_id=dev, device_id_type=MESH)

    def landed(dst, ss, rs):
        remote(dst, dst, ss, rs, at_c).wait_recv()

    barrier = pltpu.get_barrier_semaphore()
    others = range(1, NZ * NY)
    peers = [in_plane(k) for k in others] + [at_x(k) for k in (1, 2, 3)] + [at_c, at_h]
    for dev in peers:
        pl.semaphore_signal(barrier, inc=1, device_id=dev, device_id_type=MESH)
    act_in = pltpu.make_async_copy(act, act_v, loc.at[0])
    act_in.start()
    lw_in = pltpu.make_async_copy(lw, lw_v, loc.at[1])
    lw_in.start()
    op_in = pltpu.make_async_copy(op, op_v, loc.at[2])
    op_in.start()
    om_in = pltpu.make_async_copy(om, om_v, loc.at[3])
    om_in.start()

    def cot_cols(zt):
        return cot.at[:, pl.ds(pl.multiple_of(zt * COLS, COLS), COLS)]

    def cb_slot(zt, yt):
        return cb.at[zt, pl.ds(pl.multiple_of(yt * TOK, TOK), TOK)]

    cot_in = pltpu.make_async_copy(cot_cols(z), cb_slot(z, y), loc.at[4])
    cot_in.start()
    pl.semaphore_wait(barrier, len(peers))

    sends = []

    def send(*args):
        cp = remote(*args)
        cp.start()
        sends.append(cp)

    planes = (z, 1 + z % 2, (2 + 3 * z) % 5, 3 - 3 * (z // 2))

    def plane_dev(i):
        return (rep, planes[i] * 4 + y)

    def c1_send(i):
        send(cot_cols(planes[i]), cb_slot(z, y), c1s.at[i - 1], c1r.at[z], plane_dev(i))

    def c1_land(i):
        landed(cb_slot(planes[i], y), c1s.at[i - 1], c1r.at[planes[i]])

    def cb_half(zt, yt, h):
        return cb.at[zt, pl.ds(pl.multiple_of(yt * TOK + h * (TOK // 2), TOK // 2), TOK // 2)]

    def c2_send(s):
        src = cot_cols(z) if s == 0 else cb_slot(planes[s], y)
        send(src, cb_slot(planes[s], y), c2s.at[s, 0], c2r.at[s, 0], at_y(1))
        send(src, cb_slot(planes[s], y), c2s.at[s, 1], c2r.at[s, 1], at_y(3))

    def c2_pass(s):
        for i, k in ((0, 3), (1, 1)):
            landed(cb_slot(planes[s], (y + k) % 4), c2s.at[s, i], c2r.at[s, i])
            piece = cb_half(planes[s], (y + k) % 4, i)
            send(piece, piece, c2s.at[s, 2 + i], c2r.at[s, 2 + i], at_y(4 - k))

    def c2_land(s):
        for i in (0, 1):
            landed(cb_half(planes[s], (y + 2) % 4, i), c2s.at[s, 2 + i], c2r.at[s, 2 + i])

    def at_cols(q, zt, yt):
        return at[q].at[zt, :, pl.ds(pl.multiple_of(yt * TOK, TOK), TOK)]

    def a1_in():
        act_in.wait()

    def a1_send(q):
        size, start = CHUNKS[q], STARTS[q]
        for k in (2, 1, 3, 0):
            col = pl.multiple_of(((y + k) % 4) * ROWS + start, 128)
            block = act_v[:, pl.ds(col, size)].T
            if k == 0:
                at[q][z, :, pl.ds(pl.multiple_of(y * TOK, TOK), TOK)] = block
            else:
                act_t[k - 1, pl.ds(start, size)] = block
                send(act_t.at[k - 1, pl.ds(start, size)], at_cols(q, z, y), a1s.at[q, k - 1], a1r.at[q, k - 1], at_y(k))

    def a1_land(q):
        for k in (1, 2, 3):
            landed(at_cols(q, z, (y + 4 - k) % 4), a1s.at[q, k - 1], a1r.at[q, k - 1])

    def own_up(q):
        remote(at[q].at[z], at[q].at[z], a2us.at[q, 0], a2ur.at[q, 0], up).start()

    def own_down(q):
        remote(at[q].at[z], at[q].at[z], a2ds.at[q, 0], a2dr.at[q, 0], down).start()

    def own_out(q):
        pl.when((z == 0) | (z == 2))(lambda: own_up(q))
        pl.when((z == 1) | (z == 3))(lambda: own_down(q))

    def own_in(q):
        pl.when(z == 1)(lambda: own_up(q))
        pl.when(z == 2)(lambda: own_down(q))

    def rs_core():
        send(lw.at[:, 1 - c], rsc, rcs, rcr, at_c)

    def rs_x():
        lw_in.wait()
        landed(rsc, rcs, rcr)

        @pl.loop(0, NX * NH)
        def _(i):
            rss[i] = (lw_v[i, c].astype(F32) + rsc[i].astype(F32)).astype(BF16)

        for k in (2, 1, 3):
            send(rss.at[pl.ds(2 * ((x + k) % 4), 2)], rsx.at[pl.ds(2 * x, 2)], rxs.at[k - 1], rxr.at[k - 1], at_x(k))

    def over_x(h):
        total = rss[2 * x + h].astype(F32)
        for k in (1, 2, 3):
            total += rsx[2 * ((x + k) % 4) + h].astype(F32)
        return total

    def rs_h():
        for k in (1, 2, 3):
            landed(rsx.at[pl.ds(2 * ((x + 4 - k) % 4), 2)], rxs.at[k - 1], rxr.at[k - 1])
        zs[...] = over_x(1 - zh).astype(BF16)
        send(zs, zr, zhs, zhr, at_h)
        part[...] = over_x(zh)

    def from_below(q, d):
        slot = at[q].at[lax.max(z - d, 0)]
        landed(slot, a2us.at[q, d - 1], a2ur.at[q, d - 1])
        return slot

    def from_above(q, d):
        slot = at[q].at[lax.min(z + d, 3)]
        landed(slot, a2ds.at[q, d - 1], a2dr.at[q, d - 1])
        return slot

    def pass_up(q, d):
        slot = from_below(q, d)
        remote(slot, slot, a2us.at[q, d], a2ur.at[q, d], up).start()

    def pass_down(q, d):
        slot = from_above(q, d)
        remote(slot, slot, a2ds.at[q, d], a2dr.at[q, d], down).start()

    def pass_in(q):
        pl.when(z == 1)(lambda: pass_up(q, 1))
        pl.when(z == 2)(lambda: pass_down(q, 1))

    def pass_out(q, d):
        pl.when(z == 2)(lambda: pass_up(q, d))
        pl.when(z == 1)(lambda: pass_down(q, d))

    def a2_land(q):
        @pl.when(z == 3)
        def _():
            for d in (1, 2, 3):
                from_below(q, d)

        @pl.when(z == 0)
        def _():
            for d in (1, 2, 3):
                from_above(q, d)

    def forwarded(q):
        for d in (0, 1, 2):

            @pl.when((z < 3) & (z >= d))
            def _():
                slot = at[q].at[lax.max(z - d, 0)]
                remote(slot, slot, a2us.at[q, d], a2ur.at[q, d], up).wait_send()

            @pl.when((z > 0) & (z <= 3 - d))
            def _():
                slot = at[q].at[lax.min(z + d, 3)]
                remote(slot, slot, a2ds.at[q, d], a2dr.at[q, d], down).wait_send()

    def plow_at(xt, ht, ct):
        return plow.at[xt * 2 + ht, ct]

    def update():
        op_in.wait()
        om_in.wait()
        landed(zr, zhs, zhr)
        outer = op_v[...]
        delta = outer - (part[...] + zr[...].astype(F32)) * (1.0 / 16.0)
        moment = 0.9 * om_v[...] + delta
        param = outer - 0.7 * (delta + 0.9 * moment)
        mn_v[...] = moment
        pn_v[...] = param
        plow[x * 2 + zh, c] = param.astype(BF16)
        mine = plow_at(x, zh, c)
        send(mine, mine, gzs, gzr, at_h)
        for k in (2, 1, 3):
            send(mine, mine, gxs.at[0, k - 1], gxr.at[0, k - 1], at_x(k))
        for v, o, s in ((pn_v, pn_out, 5), (mn_v, mn_out, 6)):
            pltpu.make_async_copy(v, o, loc.at[s]).start()

    def spread_h():
        other = plow_at(x, 1 - zh, c)
        landed(other, gzs, gzr)
        for k in (2, 1, 3):
            send(other, other, gxs.at[1, k - 1], gxr.at[1, k - 1], at_x(k))

    def plow_own():
        return pltpu.make_async_copy(plow.at[:, c], plow_out.at[:, c], loc.at[7])

    def spread_c():
        for h in (0, 1):
            for k in (1, 2, 3):
                landed(plow_at((x + 4 - k) % 4, zh if h == 0 else 1 - zh, c), gxs.at[h, k - 1], gxr.at[h, k - 1])
        send(plow.at[:, c], plow_out.at[:, c], gcs, gcr, at_c)
        plow_own().start()

    def gr_rows(yt, q):
        return g_out.at[pl.ds(pl.multiple_of(yt * ROWS + STARTS[q], 128), CHUNKS[q])]

    def gradient(q):
        if q == 0:
            cot_in.wait()
        size = CHUNKS[q]
        rows = pl.ds(0, size)
        for g in range(NZ):
            term = jnp.dot(at[q][g], cb[g], preferred_element_type=F32)
            if g == 0:
                acc[rows] = term
            else:
                acc[rows] += term

        @pl.loop(0, NY)
        def _(i):
            j = (y + 1 + i) % 4
            total = acc[rows, pl.ds(pl.multiple_of(j * OWN, OWN), OWN)]
            sq[...] += jnp.sum((total * total).reshape(size // 8, 8, OWN), axis=0)
            gs[i, pl.ds(STARTS[q], size)] = total.astype(BF16)

    def own_rows(q):
        return pltpu.make_async_copy(gs.at[3, pl.ds(STARTS[q], CHUNKS[q])], gr_rows(y, q), gos.at[q])

    def g_send(q):
        for i in (1, 0, 2):
            send(gs.at[i, pl.ds(STARTS[q], CHUNKS[q])], gr_rows(y, q), gss.at[q, i], grs.at[q, i], at_y(i + 1))
        own_rows(q).start()

    def g_land(q):
        own_rows(q).wait()
        for i in range(3):
            landed(gr_rows((y + 3 - i) % 4, q), gss.at[q, i], grs.at[q, i])

    def squares_send():
        for i, k in enumerate(others):
            send(sq, sqs.at[i], qss.at[i], qsr.at[i], in_plane(k))

    def squares_land():
        for i in range(len(others)):
            landed(sqs.at[i], qss.at[i], qsr.at[i])

    def finish():
        square = sq[...]
        for i in range(len(others)):
            square += sqs[i]
        square = jnp.sum(square, axis=(0, 1), keepdims=True)
        scale_out[...] = jnp.broadcast_to(0.125 / jnp.sqrt(square * (1.0 / (D * FF)) + 1e-6), scale_out.shape)
        landed(plow_out.at[:, 1 - c], gcs, gcr)
        plow_own().wait()

    sq[...] = jnp.zeros_like(sq)
    steps = [
        (c1_send, 1), (c1_send, 2), (c1_send, 3), (rs_core,), (a1_in,), (a1_send, 0), (a1_send, 1), (a1_send, 2),
        (a1_send, 3), (a1_send, 4), (a1_send, 5), (a1_send, 6), (a1_send, 7), (c2_send, 0), (rs_x,), (a1_land, 0),
        (own_out, 0), (own_in, 0), (a1_land, 1), (own_out, 1), (own_in, 1), (a1_land, 2), (own_out, 2), (a1_land, 3),
        (own_out, 3), (a1_land, 4), (own_out, 4), (a1_land, 5), (own_out, 5), (a1_land, 6), (own_out, 6), (a1_land, 7),
        (own_out, 7), (c1_land, 1), (c2_send, 1), (c2_pass, 0), (rs_h,), (c1_land, 2), (c2_send, 2), (pass_in, 0),
        (own_in, 2), (c1_land, 3), (c2_send, 3), (pass_in, 1), (own_in, 3), (pass_in, 2), (own_in, 4), (pass_in, 3),
        (own_in, 5), (c2_pass, 1), (pass_in, 4), (own_in, 6), (pass_out, 0, 1), (pass_in, 5), (own_in, 7), (pass_in, 6),
        (pass_out, 0, 2), (pass_out, 1, 1), (pass_in, 7), (c2_pass, 2), (pass_out, 1, 2), (pass_out, 2, 1), (c2_pass, 3), (update,),
        (pass_out, 2, 2), (pass_out, 3, 1), (c2_land, 0), (c2_land, 1), (c2_land, 2), (c2_land, 3), (pass_out, 3, 2), (pass_out, 4, 1),
        (a2_land, 0), (gradient, 0), (g_send, 0), (a2_land, 1), (gradient, 1), (g_send, 1), (pass_out, 4, 2), (pass_out, 5, 1),
        (a2_land, 2), (gradient, 2), (g_send, 2), (pass_out, 5, 2), (pass_out, 6, 1), (spread_h,), (a2_land, 3), (gradient, 3),
        (g_send, 3), (pass_out, 6, 2), (pass_out, 7, 1), (a2_land, 4), (gradient, 4), (g_send, 4), (pass_out, 7, 2), (a2_land, 5),
        (gradient, 5), (g_send, 5), (spread_c,), (a2_land, 6), (gradient, 6), (g_send, 6), (a2_land, 7), (gradient, 7),
        (squares_send,), (g_send, 7), (squares_land,), (g_land, 0), (g_land, 1), (g_land, 2), (g_land, 3), (g_land, 4),
        (g_land, 5), (g_land, 6), (g_land, 7), (finish,),
    ]
    for step, *args in steps:
        step(*args)

    for cp in sends:
        cp.wait_send()
    for q in range(Q):
        forwarded(q)
    for v, o, s in ((pn_v, pn_out, 5), (mn_v, mn_out, 6)):
        pltpu.make_async_copy(v, o, loc.at[s]).wait()


def merge(scale, g, lw, low, pn, mn, merged, pn_out, mn_out, out_v, out_sem):
    thin = [pltpu.make_async_copy(src, dst, out_sem.at[n]) for n, (src, dst) in enumerate(((pn, pn_out), (mn, mn_out)))]
    for cp in thin:
        cp.start()

    @pl.loop(0, D // PIECE)
    def _(i):
        rows = pl.ds(pl.multiple_of(i * PIECE, PIECE), PIECE)
        base = lw[rows].astype(F32) + low[rows].astype(F32)
        out_v[rows] = (0.5 * base - scale[0:1, 0:1] * g[rows].astype(F32)).astype(BF16)
        pltpu.make_async_copy(out_v.at[rows], merged.at[rows], out_sem.at[2]).start()

    pltpu.make_async_copy(out_v, merged, out_sem.at[2]).wait()
    for cp in thin:
        cp.wait()


def local(activations, cotangent, local_weight, outer_param, outer_moment):
    dma = pltpu.SemaphoreType.DMA
    state = (BLOCK, OWN)
    half = (NX * NH, BLOCK, OWN)
    whole = (NX * NH, NC, BLOCK, OWN)
    scratch = [pltpu.VMEM((NZ, size, NY * TOK), BF16) for size in CHUNKS]
    scratch += [
        pltpu.VMEM((TOK, D), BF16),
        pltpu.VMEM((3, ROWS, TOK), BF16),
        pltpu.VMEM((NZ, NY * TOK, COLS), BF16),
        pltpu.VMEM((NY, ROWS, OWN), BF16),
        pltpu.VMEM(whole, BF16),
        pltpu.VMEM(half, BF16),
        pltpu.VMEM(half, BF16),
        pltpu.VMEM(half, BF16),
        pltpu.VMEM(state, BF16),
        pltpu.VMEM(state, BF16),
        pltpu.VMEM(state, F32),
        pltpu.VMEM(whole, BF16),
        pltpu.VMEM(state, F32),
        pltpu.VMEM(state, F32),
        pltpu.VMEM(state, F32),
        pltpu.VMEM(state, F32),
        pltpu.VMEM((8, OWN), F32),
        pltpu.VMEM((NZ * NY - 1, 8, OWN), F32),
        pltpu.VMEM((max(CHUNKS), COLS), F32),
    ]
    scratch += [dma((8,)), dma((Q,))]
    scratch += [dma((Q, 3))] * 6
    scratch += [dma((3,)), dma((4,))] + [dma((4, 4))] * 2 + [dma((Q, 3))] * 2
    scratch += [dma(())] * 2 + [dma((3,))] * 2 + [dma(())] * 4
    scratch += [dma((2, 3))] * 2 + [dma(())] * 2 + [dma((NZ * NY - 1,))] * 2
    grad, low, scale, param_new, moment_new = pl.pallas_call(
        exchange,
        out_shape=(
            pltpu.VMEM((D, OWN), BF16),
            pltpu.VMEM(whole, BF16),
            pltpu.VMEM((8, 128), F32),
            pltpu.VMEM(state, F32),
            pltpu.VMEM(state, F32),
        ),
        in_specs=[pl.BlockSpec(memory_space=pl.ANY)] * 5,
        out_specs=[pl.BlockSpec(memory_space=pl.ANY)] * 2 + [pl.BlockSpec(memory_space=pltpu.VMEM)] + [pl.BlockSpec(memory_space=pl.ANY)] * 2,
        scratch_shapes=scratch,
        compiler_params=pltpu.CompilerParams(collective_id=0, has_side_effects=True, vmem_limit_bytes=36 * 2**20),
        name="exchange",
    )(*(pltpu.with_memory_space_constraint(a, pltpu.HBM) for a in (activations[0], cotangent[0], local_weight.reshape(whole), outer_param, outer_moment)))
    merged, param_new, moment_new = pl.pallas_call(
        merge,
        out_shape=(
            jax.ShapeDtypeStruct((D, OWN), BF16),
            jax.ShapeDtypeStruct(state, F32),
            jax.ShapeDtypeStruct(state, F32),
        ),
        in_specs=[pl.BlockSpec(memory_space=pltpu.VMEM)] * 6,
        out_specs=[pl.BlockSpec(memory_space=pl.ANY)] * 3,
        scratch_shapes=[pltpu.VMEM((D, OWN), BF16), dma((3,))],
        compiler_params=pltpu.CompilerParams(vmem_limit_bytes=20 * 2**20),
        name="merge",
    )(scale, grad, local_weight[0], low.reshape(D, OWN), param_new, moment_new)
    return (merged[None], param_new, moment_new)


def solution(mesh):
    placed = (
        P("replica", "fsdp", None),
        P("replica", "fsdp", None),
        P("replica", None, "fsdp"),
        P("replica", "fsdp"),
        P("replica", "fsdp"),
    )
    return jax.shard_map(
        local,
        mesh=mesh,
        in_specs=placed,
        out_specs=(P("replica", None, "fsdp"), P("replica", "fsdp"), P("replica", "fsdp")),
        check_vma=False,
    )
```

```python
import functools

import jax
import jax.numpy as jnp
from jax import lax
from jax.experimental import pallas as pl
from jax.experimental.pallas import tpu as pltpu
from jax.sharding import PartitionSpec as P

MESH = pl.DeviceIdType.MESH
F32, BF16 = jnp.float32, jnp.bfloat16

NX, NH, NC, NZ, NY = 4, 2, 2, 4, 4
TOK, D, FF = 128, 4096, 6144
ROWS, COLS = D // NY, FF // NZ
OWN = COLS // NY
BLOCK = 256
PIECE = 256
CHUNKS = (128, 128, 128, 128, 128, 128, 128, 128)
STARTS = tuple(sum(CHUNKS[:q]) for q in range(len(CHUNKS)))
Q = len(CHUNKS)


def exchange(act, cot, lw, op, om, g_out, plow_out, scale_out, pn_out, mn_out, *scratch):
    at = scratch[:Q]
    (
        act_v, act_t, cb, gs, lw_v, rsc, rss, rsx, zs, zr, part, plow, op_v, om_v, pn_v, mn_v,
        sq, sqn, sqs, acc,
        loc, gos, a1s, a1r, a2us, a2ur, a2ds, a2dr, c1s, c1r, c2s, c2r, gss, grs,
        rcs, rcr, rxs, rxr, zhs, zhr, gzs, gzr, gxs, gxr, gcs, gcr, qss, qsr,
    ) = scratch[Q:]
    rep, fs = lax.axis_index("replica"), lax.axis_index("fsdp")
    x, zh, c = rep // 4, (rep // 2) % 2, rep % 2
    z, y = fs // 4, fs % 4

    def at_y(k):
        return (rep, z * 4 + (y + k) % 4)

    def in_plane(k):
        return (rep, ((z + k // 4) % 4) * 4 + (y + k % 4) % 4)

    def at_x(k):
        return (((x + k) % 4) * 4 + zh * 2 + c, fs)

    at_c = (x * 4 + zh * 2 + (1 - c), fs)
    at_h = (x * 4 + (1 - zh) * 2 + c, fs)
    up, down = (rep, lax.min(z + 1, 3) * 4 + y), (rep, lax.max(z - 1, 0) * 4 + y)

    def remote(src, dst, ss, rs, dev):
        return pltpu.make_async_remote_copy(src_ref=src, dst_ref=dst, send_sem=ss, recv_sem=rs, device_id=dev, device_id_type=MESH)

    def landed(dst, ss, rs):
        remote(dst, dst, ss, rs, at_c).wait_recv()

    barrier = pltpu.get_barrier_semaphore()
    others = range(1, NZ * NY)
    peers = [in_plane(k) for k in others] + [at_x(k) for k in (1, 2, 3)] + [at_c, at_h]
    for dev in peers:
        pl.semaphore_signal(barrier, inc=1, device_id=dev, device_id_type=MESH)
    act_in = pltpu.make_async_copy(act, act_v, loc.at[0])
    act_in.start()
    lw_in = pltpu.make_async_copy(lw, lw_v, loc.at[1])
    lw_in.start()
    op_in = pltpu.make_async_copy(op, op_v, loc.at[2])
    op_in.start()
    om_in = pltpu.make_async_copy(om, om_v, loc.at[3])
    om_in.start()

    def cot_cols(zt):
        return cot.at[:, pl.ds(pl.multiple_of(zt * COLS, COLS), COLS)]

    def cb_slot(zt, yt):
        return cb.at[zt, pl.ds(pl.multiple_of(yt * TOK, TOK), TOK)]

    cot_in = pltpu.make_async_copy(cot_cols(z), cb_slot(z, y), loc.at[4])
    cot_in.start()
    pl.semaphore_wait(barrier, len(peers))

    sends = []

    def send(*args):
        cp = remote(*args)
        cp.start()
        sends.append(cp)

    planes = (z, 1 + z % 2, (2 + 3 * z) % 5, 3 - 3 * (z // 2))

    def plane_dev(i):
        return (rep, planes[i] * 4 + y)

    def c1_send(i):
        send(cot_cols(planes[i]), cb_slot(z, y), c1s.at[i - 1], c1r.at[z], plane_dev(i))

    def c1_land(i):
        landed(cb_slot(planes[i], y), c1s.at[i - 1], c1r.at[planes[i]])

    def cb_half(zt, yt, h):
        return cb.at[zt, pl.ds(pl.multiple_of(yt * TOK + h * (TOK // 2), TOK // 2), TOK // 2)]

    def c2_send(s):
        src = cot_cols(z) if s == 0 else cb_slot(planes[s], y)
        send(src, cb_slot(planes[s], y), c2s.at[s, 0], c2r.at[s, 0], at_y(1))
        send(src, cb_slot(planes[s], y), c2s.at[s, 1], c2r.at[s, 1], at_y(3))

    def c2_pass(s):
        for i, k in ((0, 3), (1, 1)):
            landed(cb_slot(planes[s], (y + k) % 4), c2s.at[s, i], c2r.at[s, i])
            piece = cb_half(planes[s], (y + k) % 4, i)
            send(piece, piece, c2s.at[s, 2 + i], c2r.at[s, 2 + i], at_y(4 - k))

    def c2_land(s):
        for i in (0, 1):
            landed(cb_half(planes[s], (y + 2) % 4, i), c2s.at[s, 2 + i], c2r.at[s, 2 + i])

    def at_cols(q, zt, yt):
        return at[q].at[zt, :, pl.ds(pl.multiple_of(yt * TOK, TOK), TOK)]

    def a1_in():
        act_in.wait()

    def a1_send(q):
        size, start = CHUNKS[q], STARTS[q]
        for k in (2, 1, 3, 0):
            col = pl.multiple_of(((y + k) % 4) * ROWS + start, 128)
            block = act_v[:, pl.ds(col, size)].T
            if k == 0:
                at[q][z, :, pl.ds(pl.multiple_of(y * TOK, TOK), TOK)] = block
            else:
                act_t[k - 1, pl.ds(start, size)] = block
                send(act_t.at[k - 1, pl.ds(start, size)], at_cols(q, z, y), a1s.at[q, k - 1], a1r.at[q, k - 1], at_y(k))

    def a1_land(q):
        for k in (1, 2, 3):
            landed(at_cols(q, z, (y + 4 - k) % 4), a1s.at[q, k - 1], a1r.at[q, k - 1])

    def own_up(q):
        remote(at[q].at[z], at[q].at[z], a2us.at[q, 0], a2ur.at[q, 0], up).start()

    def own_down(q):
        remote(at[q].at[z], at[q].at[z], a2ds.at[q, 0], a2dr.at[q, 0], down).start()

    def own_out(q):
        pl.when((z == 0) | (z == 2))(lambda: own_up(q))
        pl.when((z == 1) | (z == 3))(lambda: own_down(q))

    def own_in(q):
        pl.when(z == 1)(lambda: own_up(q))
        pl.when(z == 2)(lambda: own_down(q))

    def rs_core():
        send(lw.at[:, 1 - c], rsc, rcs, rcr, at_c)

    def rs_x():
        lw_in.wait()
        landed(rsc, rcs, rcr)

        @pl.loop(0, NX * NH)
        def _(i):
            rss[i] = (lw_v[i, c].astype(F32) + rsc[i].astype(F32)).astype(BF16)

        for k in (2, 1, 3):
            send(rss.at[pl.ds(2 * ((x + k) % 4), 2)], rsx.at[pl.ds(2 * x, 2)], rxs.at[k - 1], rxr.at[k - 1], at_x(k))

    def over_x(h):
        total = rss[2 * x + h].astype(F32)
        for k in (1, 2, 3):
            total += rsx[2 * ((x + k) % 4) + h].astype(F32)
        return total

    def rs_h():
        for k in (1, 2, 3):
            landed(rsx.at[pl.ds(2 * ((x + 4 - k) % 4), 2)], rxs.at[k - 1], rxr.at[k - 1])
        zs[...] = over_x(1 - zh).astype(BF16)
        send(zs, zr, zhs, zhr, at_h)
        part[...] = over_x(zh)

    def from_below(q, d):
        slot = at[q].at[lax.max(z - d, 0)]
        landed(slot, a2us.at[q, d - 1], a2ur.at[q, d - 1])

    def from_above(q, d):
        slot = at[q].at[lax.min(z + d, 3)]
        landed(slot, a2ds.at[q, d - 1], a2dr.at[q, d - 1])

    def pass_up(q, d):
        slot = at[q].at[lax.max(z - d, 0)]
        from_below(q, d)
        remote(slot, slot, a2us.at[q, d], a2ur.at[q, d], up).start()

    def pass_down(q, d):
        slot = at[q].at[lax.min(z + d, 3)]
        from_above(q, d)
        remote(slot, slot, a2ds.at[q, d], a2dr.at[q, d], down).start()

    def pass_in(q):
        pl.when(z == 1)(lambda: pass_up(q, 1))
        pl.when(z == 2)(lambda: pass_down(q, 1))

    def pass_out(q, d):
        pl.when(z == 2)(lambda: pass_up(q, d))
        pl.when(z == 1)(lambda: pass_down(q, d))

    def forwarded(q):
        for d in (0, 1, 2):

            @pl.when((z < 3) & (z >= d))
            def _():
                slot = at[q].at[lax.max(z - d, 0)]
                remote(slot, slot, a2us.at[q, d], a2ur.at[q, d], up).wait_send()

            @pl.when((z > 0) & (z <= 3 - d))
            def _():
                slot = at[q].at[lax.min(z + d, 3)]
                remote(slot, slot, a2ds.at[q, d], a2dr.at[q, d], down).wait_send()

    def plow_at(xt, ht, ct):
        return plow.at[xt * 2 + ht, ct]

    def update():
        op_in.wait()
        om_in.wait()
        landed(zr, zhs, zhr)
        outer = op_v[...]
        delta = outer - (part[...] + zr[...].astype(F32)) * (1.0 / 16.0)
        moment = 0.9 * om_v[...] + delta
        param = outer - 0.7 * (delta + 0.9 * moment)
        mn_v[...] = moment
        pn_v[...] = param
        plow[x * 2 + zh, c] = param.astype(BF16)
        mine = plow_at(x, zh, c)
        send(mine, mine, gzs, gzr, at_h)
        for k in (2, 1, 3):
            send(mine, mine, gxs.at[0, k - 1], gxr.at[0, k - 1], at_x(k))
        for v, o, s in ((pn_v, pn_out, 5), (mn_v, mn_out, 6)):
            pltpu.make_async_copy(v, o, loc.at[s]).start()

    def spread_h():
        other = plow_at(x, 1 - zh, c)
        landed(other, gzs, gzr)
        for k in (2, 1, 3):
            send(other, other, gxs.at[1, k - 1], gxr.at[1, k - 1], at_x(k))

    def plow_own():
        return pltpu.make_async_copy(plow.at[:, c], plow_out.at[:, c], loc.at[7])

    def spread_c():
        for h in (0, 1):
            for k in (1, 2, 3):
                landed(plow_at((x + 4 - k) % 4, zh if h == 0 else 1 - zh, c), gxs.at[h, k - 1], gxr.at[h, k - 1])
        send(plow.at[:, c], plow_out.at[:, c], gcs, gcr, at_c)
        plow_own().start()

    def gr_rows(yt, q):
        return g_out.at[pl.ds(pl.multiple_of(yt * ROWS + STARTS[q], 128), CHUNKS[q])]

    def gradient(q):
        if q == 0:
            cot_in.wait()
        size = CHUNKS[q]
        rows = pl.ds(0, size)
        for d in range(NZ):
            if d > 0:
                pl.when(z == 3)(lambda: from_below(q, d))
                pl.when(z == 0)(lambda: from_above(q, d))
            term = jnp.dot(at[q][planes[d]], cb[planes[d]], preferred_element_type=F32)
            if d == 0:
                acc[rows] = term
            else:
                acc[rows] += term

        @pl.loop(0, NY)
        def _(i):
            j = (y + 1 + i) % 4
            total = acc[rows, pl.ds(pl.multiple_of(j * OWN, OWN), OWN)]
            sq[...] += jnp.sum((total * total).reshape(size // 8, 8, OWN), axis=0)
            gs[i, pl.ds(STARTS[q], size)] = total.astype(BF16)

    def own_rows(q):
        return pltpu.make_async_copy(gs.at[3, pl.ds(STARTS[q], CHUNKS[q])], gr_rows(y, q), gos.at[q])

    def g_send(q):
        for i in (1, 0, 2):
            send(gs.at[i, pl.ds(STARTS[q], CHUNKS[q])], gr_rows(y, q), gss.at[q, i], grs.at[q, i], at_y(i + 1))
        own_rows(q).start()

    def g_land(q):
        own_rows(q).wait()
        for i in range(3):
            landed(gr_rows((y + 3 - i) % 4, q), gss.at[q, i], grs.at[q, i])

    def drain(n):
        for cp in sends[:n]:
            cp.wait_send()
        del sends[:n]

    def squares_send():
        sqn[...] = sq[:, 0:128] + sq[:, 128:256] + sq[:, 256:384]
        for i, k in enumerate(others):
            send(sqn, sqs.at[i], qss.at[i], qsr.at[i], in_plane(k))

    def squares_land():
        for i in range(len(others)):
            landed(sqs.at[i], qss.at[i], qsr.at[i])

    def finish():
        square = sqn[...]
        for i in range(len(others)):
            square += sqs[i]
        square = jnp.sum(square, axis=(0, 1), keepdims=True)
        scale_out[...] = jnp.broadcast_to(0.125 / jnp.sqrt(square * (1.0 / (D * FF)) + 1e-6), scale_out.shape)
        landed(plow_out.at[:, 1 - c], gcs, gcr)
        plow_own().wait()

    sq[...] = jnp.zeros_like(sq)
    steps = [
        (c1_send, 1), (c1_send, 2), (c1_send, 3), (rs_core,), (a1_in,), (a1_send, 0), (a1_send, 1), (a1_send, 2),
        (a1_send, 3), (a1_send, 4), (a1_send, 5), (a1_send, 6), (a1_send, 7), (c2_send, 0), (rs_x,), (a1_land, 0),
        (own_out, 0), (own_in, 0), (a1_land, 1), (own_out, 1), (own_in, 1), (a1_land, 2), (own_out, 2), (a1_land, 3),
        (own_out, 3), (a1_land, 4), (own_out, 4), (a1_land, 5), (own_out, 5), (a1_land, 6), (own_out, 6), (a1_land, 7),
        (own_out, 7), (c1_land, 1), (c2_send, 1), (c2_pass, 0), (rs_h,), (c1_land, 2), (c2_send, 2), (pass_in, 0),
        (own_in, 2), (c1_land, 3), (c2_send, 3), (pass_in, 1), (own_in, 3), (pass_in, 2), (own_in, 4), (pass_in, 3),
        (own_in, 5), (c2_pass, 1), (pass_in, 4), (own_in, 6), (pass_out, 0, 1), (pass_in, 5), (own_in, 7), (pass_in, 6),
        (pass_out, 0, 2), (pass_out, 1, 1), (pass_in, 7), (c2_pass, 2), (pass_out, 1, 2), (pass_out, 2, 1), (c2_pass, 3), (update,),
        (pass_out, 2, 2), (pass_out, 3, 1), (c2_land, 0), (c2_land, 1), (c2_land, 2), (c2_land, 3), (pass_out, 3, 2), (pass_out, 4, 1),
        (gradient, 0), (g_send, 0), (gradient, 1), (g_send, 1), (pass_out, 4, 2), (pass_out, 5, 1), (gradient, 2), (g_send, 2),
        (pass_out, 5, 2), (pass_out, 6, 1), (spread_h,), (gradient, 3), (g_send, 3), (pass_out, 6, 2), (pass_out, 7, 1), (gradient, 4),
        (g_send, 4), (pass_out, 7, 2), (gradient, 5), (g_send, 5), (spread_c,), (gradient, 6), (g_send, 6), (forwarded, 0),
        (forwarded, 1), (forwarded, 2), (forwarded, 3), (forwarded, 4), (forwarded, 5), (drain, -6), (g_land, 0), (g_land, 1),
        (g_land, 2), (g_land, 3), (g_land, 4), (gradient, 7), (squares_send,), (g_send, 7), (squares_land,), (g_land, 5),
        (g_land, 6), (g_land, 7), (finish,),
    ]
    for step, *args in steps:
        step(*args)

    for cp in sends:
        cp.wait_send()
    for q in range(Q - 2, Q):
        forwarded(q)
    for v, o, s in ((pn_v, pn_out, 5), (mn_v, mn_out, 6)):
        pltpu.make_async_copy(v, o, loc.at[s]).wait()


def merge(scale, g, lw, low, pn, mn, merged, pn_out, mn_out, out_v, out_sem):
    thin = [pltpu.make_async_copy(src, dst, out_sem.at[n]) for n, (src, dst) in enumerate(((pn, pn_out), (mn, mn_out)))]
    for cp in thin:
        cp.start()

    @pl.loop(0, D // PIECE)
    def _(i):
        rows = pl.ds(pl.multiple_of(i * PIECE, PIECE), PIECE)
        base = lw[rows].astype(F32) + low[rows].astype(F32)
        out_v[rows] = (0.5 * base - scale[0:1, 0:1] * g[rows].astype(F32)).astype(BF16)
        pltpu.make_async_copy(out_v.at[rows], merged.at[rows], out_sem.at[2]).start()

    pltpu.make_async_copy(out_v, merged, out_sem.at[2]).wait()
    for cp in thin:
        cp.wait()


def local(activations, cotangent, local_weight, outer_param, outer_moment):
    dma = pltpu.SemaphoreType.DMA
    state = (BLOCK, OWN)
    half = (NX * NH, BLOCK, OWN)
    whole = (NX * NH, NC, BLOCK, OWN)
    scratch = [pltpu.VMEM((NZ, size, NY * TOK), BF16) for size in CHUNKS]
    scratch += [
        pltpu.VMEM((TOK, D), BF16),
        pltpu.VMEM((3, ROWS, TOK), BF16),
        pltpu.VMEM((NZ, NY * TOK, COLS), BF16),
        pltpu.VMEM((NY, ROWS, OWN), BF16),
        pltpu.VMEM(whole, BF16),
        pltpu.VMEM(half, BF16),
        pltpu.VMEM(half, BF16),
        pltpu.VMEM(half, BF16),
        pltpu.VMEM(state, BF16),
        pltpu.VMEM(state, BF16),
        pltpu.VMEM(state, F32),
        pltpu.VMEM(whole, BF16),
        pltpu.VMEM(state, F32),
        pltpu.VMEM(state, F32),
        pltpu.VMEM(state, F32),
        pltpu.VMEM(state, F32),
        pltpu.VMEM((8, OWN), F32),
        pltpu.VMEM((8, 128), F32),
        pltpu.VMEM((NZ * NY - 1, 8, 128), F32),
        pltpu.VMEM((max(CHUNKS), COLS), F32),
    ]
    scratch += [dma((8,)), dma((Q,))]
    scratch += [dma((Q, 3))] * 6
    scratch += [dma((3,)), dma((4,))] + [dma((4, 4))] * 2 + [dma((Q, 3))] * 2
    scratch += [dma(())] * 2 + [dma((3,))] * 2 + [dma(())] * 4
    scratch += [dma((2, 3))] * 2 + [dma(())] * 2 + [dma((NZ * NY - 1,))] * 2
    grad, low, scale, param_new, moment_new = pl.pallas_call(
        exchange,
        out_shape=(
            pltpu.VMEM((D, OWN), BF16),
            pltpu.VMEM(whole, BF16),
            pltpu.VMEM((8, 128), F32),
            pltpu.VMEM(state, F32),
            pltpu.VMEM(state, F32),
        ),
        in_specs=[pl.BlockSpec(memory_space=pl.ANY)] * 5,
        out_specs=[pl.BlockSpec(memory_space=pl.ANY)] * 2 + [pl.BlockSpec(memory_space=pltpu.VMEM)] + [pl.BlockSpec(memory_space=pl.ANY)] * 2,
        scratch_shapes=scratch,
        compiler_params=pltpu.CompilerParams(collective_id=0, has_side_effects=True, vmem_limit_bytes=36 * 2**20),
        name="exchange",
    )(*(pltpu.with_memory_space_constraint(a, pltpu.HBM) for a in (activations[0], cotangent[0], local_weight.reshape(whole), outer_param, outer_moment)))
    merged, param_new, moment_new = pl.pallas_call(
        merge,
        out_shape=(
            jax.ShapeDtypeStruct((D, OWN), BF16),
            jax.ShapeDtypeStruct(state, F32),
            jax.ShapeDtypeStruct(state, F32),
        ),
        in_specs=[pl.BlockSpec(memory_space=pltpu.VMEM)] * 6,
        out_specs=[pl.BlockSpec(memory_space=pl.ANY)] * 3,
        scratch_shapes=[pltpu.VMEM((D, OWN), BF16), dma((3,))],
        compiler_params=pltpu.CompilerParams(vmem_limit_bytes=20 * 2**20),
        name="merge",
    )(scale, grad, local_weight[0], low.reshape(D, OWN), param_new, moment_new)
    return (merged[None], param_new, moment_new)


def solution(mesh):
    placed = (
        P("replica", "fsdp", None),
        P("replica", "fsdp", None),
        P("replica", None, "fsdp"),
        P("replica", "fsdp"),
        P("replica", "fsdp"),
    )
    return jax.shard_map(
        local,
        mesh=mesh,
        in_specs=placed,
        out_specs=(P("replica", None, "fsdp"), P("replica", "fsdp"), P("replica", "fsdp")),
        check_vma=False,
    )
```

```python
import functools

import jax
import jax.numpy as jnp
from jax import lax
from jax.experimental import pallas as pl
from jax.experimental.pallas import tpu as pltpu
from jax.sharding import PartitionSpec as P

MESH = pl.DeviceIdType.MESH
F32, BF16 = jnp.float32, jnp.bfloat16

NX, NH, NC, NZ, NY = 4, 2, 2, 4, 4
TOK, D, FF = 128, 4096, 6144
ROWS, COLS = D // NY, FF // NZ
OWN = COLS // NY
BLOCK = 256
PIECE = 512
CHUNKS = (128, 128, 128, 128, 128, 128, 128, 128)
STARTS = tuple(sum(CHUNKS[:q]) for q in range(len(CHUNKS)))
Q = len(CHUNKS)


def exchange(act, cot, lw, op, om, g_out, plow_out, scale_out, pn_out, mn_out, *scratch):
    at = scratch[:Q]
    (
        act_v, act_t, cb, gs, lw_v, rsc, rss, rsx, zs, zr, part, plow, op_v, om_v, pn_v, mn_v,
        sq, sqn, sqs, acc,
        loc, gos, a1s, a1r, a2us, a2ur, a2ds, a2dr, c1s, c1r, c2s, c2r, gss, grs,
        rcs, rcr, rxs, rxr, zhs, zhr, gzs, gzr, gxs, gxr, gcs, gcr, qss, qsr,
    ) = scratch[Q:]
    rep, fs = lax.axis_index("replica"), lax.axis_index("fsdp")
    x, zh, c = rep // 4, (rep // 2) % 2, rep % 2
    z, y = fs // 4, fs % 4

    def at_y(k):
        return (rep, z * 4 + (y + k) % 4)

    def in_plane(k):
        return (rep, ((z + k // 4) % 4) * 4 + (y + k % 4) % 4)

    def at_x(k):
        return (((x + k) % 4) * 4 + zh * 2 + c, fs)

    at_c = (x * 4 + zh * 2 + (1 - c), fs)
    at_h = (x * 4 + (1 - zh) * 2 + c, fs)
    up, down = (rep, lax.min(z + 1, 3) * 4 + y), (rep, lax.max(z - 1, 0) * 4 + y)

    def remote(src, dst, ss, rs, dev):
        return pltpu.make_async_remote_copy(src_ref=src, dst_ref=dst, send_sem=ss, recv_sem=rs, device_id=dev, device_id_type=MESH)

    def landed(dst, ss, rs):
        remote(dst, dst, ss, rs, at_c).wait_recv()

    barrier = pltpu.get_barrier_semaphore()
    others = range(1, NZ * NY)
    peers = [in_plane(k) for k in others] + [at_x(k) for k in (1, 2, 3)] + [at_c, at_h]
    for dev in peers:
        pl.semaphore_signal(barrier, inc=1, device_id=dev, device_id_type=MESH)
    act_in = pltpu.make_async_copy(act, act_v, loc.at[0])
    act_in.start()
    lw_in = pltpu.make_async_copy(lw, lw_v, loc.at[1])
    lw_in.start()
    op_in = pltpu.make_async_copy(op, op_v, loc.at[2])
    op_in.start()
    om_in = pltpu.make_async_copy(om, om_v, loc.at[3])
    om_in.start()

    def cot_cols(zt):
        return cot.at[:, pl.ds(pl.multiple_of(zt * COLS, COLS), COLS)]

    def cb_slot(zt, yt):
        return cb.at[zt, pl.ds(pl.multiple_of(yt * TOK, TOK), TOK)]

    cot_in = pltpu.make_async_copy(cot_cols(z), cb_slot(z, y), loc.at[4])
    cot_in.start()
    pl.semaphore_wait(barrier, len(peers))

    sends = []

    def send(*args):
        cp = remote(*args)
        cp.start()
        sends.append(cp)

    planes = (z, 1 + z % 2, (2 + 3 * z) % 5, 3 - 3 * (z // 2))

    def plane_dev(i):
        return (rep, planes[i] * 4 + y)

    def c1_send(i):
        send(cot_cols(planes[i]), cb_slot(z, y), c1s.at[i - 1], c1r.at[z], plane_dev(i))

    def c1_land(i):
        landed(cb_slot(planes[i], y), c1s.at[i - 1], c1r.at[planes[i]])

    def cb_half(zt, yt, h):
        return cb.at[zt, pl.ds(pl.multiple_of(yt * TOK + h * (TOK // 2), TOK // 2), TOK // 2)]

    def c2_send(s):
        src = cot_cols(z) if s == 0 else cb_slot(planes[s], y)
        send(src, cb_slot(planes[s], y), c2s.at[s, 0], c2r.at[s, 0], at_y(1))
        send(src, cb_slot(planes[s], y), c2s.at[s, 1], c2r.at[s, 1], at_y(3))

    def c2_pass(s):
        for i, k in ((0, 3), (1, 1)):
            landed(cb_slot(planes[s], (y + k) % 4), c2s.at[s, i], c2r.at[s, i])
            piece = cb_half(planes[s], (y + k) % 4, i)
            send(piece, piece, c2s.at[s, 2 + i], c2r.at[s, 2 + i], at_y(4 - k))

    def c2_land(s):
        for i in (0, 1):
            landed(cb_half(planes[s], (y + 2) % 4, i), c2s.at[s, 2 + i], c2r.at[s, 2 + i])

    def at_cols(q, zt, yt):
        return at[q].at[zt, :, pl.ds(pl.multiple_of(yt * TOK, TOK), TOK)]

    def a1_in():
        act_in.wait()

    def a1_send(q):
        size, start = CHUNKS[q], STARTS[q]
        for k in (2, 1, 3, 0):
            col = pl.multiple_of(((y + k) % 4) * ROWS + start, 128)
            block = act_v[:, pl.ds(col, size)].T
            if k == 0:
                at[q][z, :, pl.ds(pl.multiple_of(y * TOK, TOK), TOK)] = block
            else:
                act_t[k - 1, pl.ds(start, size)] = block
                send(act_t.at[k - 1, pl.ds(start, size)], at_cols(q, z, y), a1s.at[q, k - 1], a1r.at[q, k - 1], at_y(k))

    def a1_land(q):
        for k in (1, 2, 3):
            landed(at_cols(q, z, (y + 4 - k) % 4), a1s.at[q, k - 1], a1r.at[q, k - 1])

    def own_up(q):
        remote(at[q].at[z], at[q].at[z], a2us.at[q, 0], a2ur.at[q, 0], up).start()

    def own_down(q):
        remote(at[q].at[z], at[q].at[z], a2ds.at[q, 0], a2dr.at[q, 0], down).start()

    def own_out(q):
        pl.when((z == 0) | (z == 2))(lambda: own_up(q))
        pl.when((z == 1) | (z == 3))(lambda: own_down(q))

    def own_in(q):
        pl.when(z == 1)(lambda: own_up(q))
        pl.when(z == 2)(lambda: own_down(q))

    def rs_core():
        send(lw.at[:, 1 - c], rsc, rcs, rcr, at_c)

    def rs_x():
        lw_in.wait()
        landed(rsc, rcs, rcr)

        @pl.loop(0, NX * NH)
        def _(i):
            rss[i] = (lw_v[i, c].astype(F32) + rsc[i].astype(F32)).astype(BF16)

        for k in (2, 1, 3):
            send(rss.at[pl.ds(2 * ((x + k) % 4), 2)], rsx.at[pl.ds(2 * x, 2)], rxs.at[k - 1], rxr.at[k - 1], at_x(k))

    def over_x(h):
        total = rss[2 * x + h].astype(F32)
        for k in (1, 2, 3):
            total += rsx[2 * ((x + k) % 4) + h].astype(F32)
        return total

    def rs_h():
        for k in (1, 2, 3):
            landed(rsx.at[pl.ds(2 * ((x + 4 - k) % 4), 2)], rxs.at[k - 1], rxr.at[k - 1])
        zs[...] = over_x(1 - zh).astype(BF16)
        send(zs, zr, zhs, zhr, at_h)
        part[...] = over_x(zh)

    def from_below(q, d):
        slot = at[q].at[lax.max(z - d, 0)]
        landed(slot, a2us.at[q, d - 1], a2ur.at[q, d - 1])

    def from_above(q, d):
        slot = at[q].at[lax.min(z + d, 3)]
        landed(slot, a2ds.at[q, d - 1], a2dr.at[q, d - 1])

    def pass_up(q, d):
        slot = at[q].at[lax.max(z - d, 0)]
        from_below(q, d)
        remote(slot, slot, a2us.at[q, d], a2ur.at[q, d], up).start()

    def pass_down(q, d):
        slot = at[q].at[lax.min(z + d, 3)]
        from_above(q, d)
        remote(slot, slot, a2ds.at[q, d], a2dr.at[q, d], down).start()

    def pass_in(q):
        pl.when(z == 1)(lambda: pass_up(q, 1))
        pl.when(z == 2)(lambda: pass_down(q, 1))

    def pass_out(q, d):
        pl.when(z == 2)(lambda: pass_up(q, d))
        pl.when(z == 1)(lambda: pass_down(q, d))

    def forwarded(q):
        for d in (0, 1, 2):

            @pl.when((z < 3) & (z >= d))
            def _():
                slot = at[q].at[lax.max(z - d, 0)]
                remote(slot, slot, a2us.at[q, d], a2ur.at[q, d], up).wait_send()

            @pl.when((z > 0) & (z <= 3 - d))
            def _():
                slot = at[q].at[lax.min(z + d, 3)]
                remote(slot, slot, a2ds.at[q, d], a2dr.at[q, d], down).wait_send()

    def plow_at(xt, ht, ct):
        return plow.at[xt * 2 + ht, ct]

    def update():
        op_in.wait()
        om_in.wait()
        landed(zr, zhs, zhr)
        outer = op_v[...]
        delta = outer - (part[...] + zr[...].astype(F32)) * (1.0 / 16.0)
        moment = 0.9 * om_v[...] + delta
        param = outer - 0.7 * (delta + 0.9 * moment)
        mn_v[...] = moment
        pn_v[...] = param
        plow[x * 2 + zh, c] = param.astype(BF16)
        mine = plow_at(x, zh, c)
        send(mine, mine, gzs, gzr, at_h)
        for k in (2, 1, 3):
            send(mine, mine, gxs.at[0, k - 1], gxr.at[0, k - 1], at_x(k))
        for v, o, s in ((pn_v, pn_out, 5), (mn_v, mn_out, 6)):
            pltpu.make_async_copy(v, o, loc.at[s]).start()

    def spread_h():
        other = plow_at(x, 1 - zh, c)
        landed(other, gzs, gzr)
        for k in (2, 1, 3):
            send(other, other, gxs.at[1, k - 1], gxr.at[1, k - 1], at_x(k))

    def plow_own():
        return pltpu.make_async_copy(plow.at[:, c], plow_out.at[:, c], loc.at[7])

    def spread_c():
        for h in (0, 1):
            for k in (1, 2, 3):
                landed(plow_at((x + 4 - k) % 4, zh if h == 0 else 1 - zh, c), gxs.at[h, k - 1], gxr.at[h, k - 1])
        send(plow.at[:, c], plow_out.at[:, c], gcs, gcr, at_c)
        plow_own().start()

    def gr_rows(yt, q):
        return g_out.at[pl.ds(pl.multiple_of(yt * ROWS + STARTS[q], 128), CHUNKS[q])]

    def gradient(q):
        if q == 0:
            cot_in.wait()
        size = CHUNKS[q]
        rows = pl.ds(0, size)
        for d in range(NZ):
            if d > 0:
                pl.when(z == 3)(lambda: from_below(q, d))
                pl.when(z == 0)(lambda: from_above(q, d))
            term = jnp.dot(at[q][planes[d]], cb[planes[d]], preferred_element_type=F32)
            if d == 0:
                acc[rows] = term
            else:
                acc[rows] += term

        @pl.loop(0, NY)
        def _(i):
            j = (y + 1 + i) % 4
            total = acc[rows, pl.ds(pl.multiple_of(j * OWN, OWN), OWN)]
            sq[...] += jnp.sum((total * total).reshape(size // 8, 8, OWN), axis=0)
            gs[i, pl.ds(STARTS[q], size)] = total.astype(BF16)

    def own_rows(q):
        return pltpu.make_async_copy(gs.at[3, pl.ds(STARTS[q], CHUNKS[q])], gr_rows(y, q), gos.at[q])

    def g_send(q):
        for i in (1, 0, 2):
            send(gs.at[i, pl.ds(STARTS[q], CHUNKS[q])], gr_rows(y, q), gss.at[q, i], grs.at[q, i], at_y(i + 1))
        own_rows(q).start()

    def g_land(q):
        own_rows(q).wait()
        for i in range(3):
            landed(gr_rows((y + 3 - i) % 4, q), gss.at[q, i], grs.at[q, i])

    def drain(n):
        for cp in sends[:n]:
            cp.wait_send()
        del sends[:n]

    def squares_send():
        sqn[...] = sq[:, 0:128] + sq[:, 128:256] + sq[:, 256:384]
        for i, k in enumerate(others):
            send(sqn, sqs.at[i], qss.at[i], qsr.at[i], in_plane(k))

    def squares_land():
        for i in range(len(others)):
            landed(sqs.at[i], qss.at[i], qsr.at[i])

    def finish():
        square = sqn[...]
        for i in range(len(others)):
            square += sqs[i]
        square = jnp.sum(square, axis=(0, 1), keepdims=True)
        scale_out[...] = jnp.broadcast_to(0.125 / jnp.sqrt(square * (1.0 / (D * FF)) + 1e-6), scale_out.shape)
        landed(plow_out.at[:, 1 - c], gcs, gcr)
        plow_own().wait()

    sq[...] = jnp.zeros_like(sq)
    steps = [
        (c1_send, 1), (c1_send, 2), (c1_send, 3), (rs_core,), (a1_in,), (a1_send, 0), (a1_send, 1), (a1_send, 2),
        (a1_send, 3), (a1_send, 4), (a1_send, 5), (a1_send, 6), (a1_send, 7), (c2_send, 0), (rs_x,), (a1_land, 0),
        (own_out, 0), (own_in, 0), (a1_land, 1), (own_out, 1), (own_in, 1), (a1_land, 2), (own_out, 2), (a1_land, 3),
        (own_out, 3), (a1_land, 4), (own_out, 4), (a1_land, 5), (own_out, 5), (a1_land, 6), (own_out, 6), (a1_land, 7),
        (own_out, 7), (c1_land, 1), (c2_send, 1), (c2_pass, 0), (rs_h,), (c1_land, 2), (c2_send, 2), (pass_in, 0),
        (own_in, 2), (c1_land, 3), (c2_send, 3), (pass_in, 1), (own_in, 3), (pass_in, 2), (own_in, 4), (pass_in, 3),
        (own_in, 5), (c2_pass, 1), (pass_in, 4), (own_in, 6), (pass_out, 0, 1), (pass_in, 5), (own_in, 7), (pass_in, 6),
        (pass_out, 0, 2), (pass_out, 1, 1), (pass_in, 7), (c2_pass, 2), (pass_out, 1, 2), (pass_out, 2, 1), (c2_pass, 3), (update,),
        (pass_out, 2, 2), (pass_out, 3, 1), (c2_land, 0), (c2_land, 1), (c2_land, 2), (c2_land, 3), (pass_out, 3, 2), (pass_out, 4, 1),
        (gradient, 0), (g_send, 0), (gradient, 1), (g_send, 1), (pass_out, 4, 2), (pass_out, 5, 1), (gradient, 2), (g_send, 2),
        (pass_out, 5, 2), (pass_out, 6, 1), (spread_h,), (gradient, 3), (g_send, 3), (pass_out, 6, 2), (pass_out, 7, 1), (gradient, 4),
        (g_send, 4), (pass_out, 7, 2), (gradient, 5), (g_send, 5), (spread_c,), (gradient, 6), (g_send, 6), (forwarded, 0),
        (forwarded, 1), (forwarded, 2), (forwarded, 3), (forwarded, 4), (forwarded, 5), (drain, -6), (g_land, 0), (g_land, 1),
        (g_land, 2), (g_land, 3), (g_land, 4), (gradient, 7), (squares_send,), (g_send, 7), (squares_land,), (g_land, 5),
        (g_land, 6), (g_land, 7), (finish,),
    ]
    for step, *args in steps:
        step(*args)

    for cp in sends:
        cp.wait_send()
    for q in range(Q - 2, Q):
        forwarded(q)
    for v, o, s in ((pn_v, pn_out, 5), (mn_v, mn_out, 6)):
        pltpu.make_async_copy(v, o, loc.at[s]).wait()


def merge(scale, g, lw, low, pn, mn, merged, pn_out, mn_out, out_v, out_sem):
    thin = [pltpu.make_async_copy(src, dst, out_sem.at[n]) for n, (src, dst) in enumerate(((pn, pn_out), (mn, mn_out)))]
    for cp in thin:
        cp.start()

    @pl.loop(0, D // PIECE)
    def _(i):
        rows = pl.ds(pl.multiple_of(i * PIECE, PIECE), PIECE)
        base = lw[rows].astype(F32) + low[rows].astype(F32)
        out_v[rows] = (0.5 * base - scale[0:1, 0:1] * g[rows].astype(F32)).astype(BF16)
        pltpu.make_async_copy(out_v.at[rows], merged.at[rows], out_sem.at[2]).start()

    pltpu.make_async_copy(out_v, merged, out_sem.at[2]).wait()
    for cp in thin:
        cp.wait()


def local(activations, cotangent, local_weight, outer_param, outer_moment):
    dma = pltpu.SemaphoreType.DMA
    state = (BLOCK, OWN)
    half = (NX * NH, BLOCK, OWN)
    whole = (NX * NH, NC, BLOCK, OWN)
    scratch = [pltpu.VMEM((NZ, size, NY * TOK), BF16) for size in CHUNKS]
    scratch += [
        pltpu.VMEM((TOK, D), BF16),
        pltpu.VMEM((3, ROWS, TOK), BF16),
        pltpu.VMEM((NZ, NY * TOK, COLS), BF16),
        pltpu.VMEM((NY, ROWS, OWN), BF16),
        pltpu.VMEM(whole, BF16),
        pltpu.VMEM(half, BF16),
        pltpu.VMEM(half, BF16),
        pltpu.VMEM(half, BF16),
        pltpu.VMEM(state, BF16),
        pltpu.VMEM(state, BF16),
        pltpu.VMEM(state, F32),
        pltpu.VMEM(whole, BF16),
        pltpu.VMEM(state, F32),
        pltpu.VMEM(state, F32),
        pltpu.VMEM(state, F32),
        pltpu.VMEM(state, F32),
        pltpu.VMEM((8, OWN), F32),
        pltpu.VMEM((8, 128), F32),
        pltpu.VMEM((NZ * NY - 1, 8, 128), F32),
        pltpu.VMEM((max(CHUNKS), COLS), F32),
    ]
    scratch += [dma((8,)), dma((Q,))]
    scratch += [dma((Q, 3))] * 6
    scratch += [dma((3,)), dma((4,))] + [dma((4, 4))] * 2 + [dma((Q, 3))] * 2
    scratch += [dma(())] * 2 + [dma((3,))] * 2 + [dma(())] * 4
    scratch += [dma((2, 3))] * 2 + [dma(())] * 2 + [dma((NZ * NY - 1,))] * 2
    grad, low, scale, param_new, moment_new = pl.pallas_call(
        exchange,
        out_shape=(
            pltpu.VMEM((D, OWN), BF16),
            pltpu.VMEM(whole, BF16),
            pltpu.VMEM((8, 128), F32),
            pltpu.VMEM(state, F32),
            pltpu.VMEM(state, F32),
        ),
        in_specs=[pl.BlockSpec(memory_space=pl.ANY)] * 5,
        out_specs=[pl.BlockSpec(memory_space=pl.ANY)] * 2 + [pl.BlockSpec(memory_space=pltpu.VMEM)] + [pl.BlockSpec(memory_space=pl.ANY)] * 2,
        scratch_shapes=scratch,
        compiler_params=pltpu.CompilerParams(collective_id=0, has_side_effects=True, vmem_limit_bytes=36 * 2**20),
        name="exchange",
    )(*(pltpu.with_memory_space_constraint(a, pltpu.HBM) for a in (activations[0], cotangent[0], local_weight.reshape(whole), outer_param, outer_moment)))
    merged, param_new, moment_new = pl.pallas_call(
        merge,
        out_shape=(
            jax.ShapeDtypeStruct((D, OWN), BF16),
            jax.ShapeDtypeStruct(state, F32),
            jax.ShapeDtypeStruct(state, F32),
        ),
        in_specs=[pl.BlockSpec(memory_space=pltpu.VMEM)] * 6,
        out_specs=[pl.BlockSpec(memory_space=pl.ANY)] * 3,
        scratch_shapes=[pltpu.VMEM((D, OWN), BF16), dma((3,))],
        compiler_params=pltpu.CompilerParams(vmem_limit_bytes=20 * 2**20),
        name="merge",
    )(scale, grad, local_weight[0], low.reshape(D, OWN), param_new, moment_new)
    return (merged[None], param_new, moment_new)


def solution(mesh):
    placed = (
        P("replica", "fsdp", None),
        P("replica", "fsdp", None),
        P("replica", None, "fsdp"),
        P("replica", "fsdp"),
        P("replica", "fsdp"),
    )
    return jax.shard_map(
        local,
        mesh=mesh,
        in_specs=placed,
        out_specs=(P("replica", None, "fsdp"), P("replica", "fsdp"), P("replica", "fsdp")),
        check_vma=False,
    )
```
